32 devices in a mesh: dp: 2 (over y), row: 4 (over z), col: 4 (over x, core).
Axes of the slice: x: 2, y: 2, z: 4, core: 2. Of those that a mesh axis runs over, the one named last changes fastest.
Arguments:
- act_in: bfloat16 [2048, 1024], P(('dp', 'col'), 'row'), may hold values from -8 to 8
- act_cot: bfloat16 [2048, 1024], P(('dp', 'col'), 'row'), may hold values from -6 to 6
- segments: int32 [2048], P(('dp', 'col')), may hold values from 0 to 7, as said below
- positions: int32 [2048], P(('dp', 'col')), may hold values from 0 to 382, as said below
- gains: float32 [2304], replicated, may hold values from 0.5 to 1.5
- gains_first: float32 [2304], replicated, may hold values from -32 to 32
- gains_second: float32 [2304], replicated, may hold values from 53.8624 to 861.7984
- query_weight: float32 [1024, 2048], P(('dp', 'col'), 'row'), may hold values from -0.1875 to 0.1875
- query_first: float32 [1024, 2048], P(('dp', 'col'), 'row'), may hold values from -4 to 4
- query_second: float32 [1024, 2048], P(('dp', 'col'), 'row'), may hold values from 4.847616 to 77.56186
- key_weight: float32 [1024, 1024], P(('dp', 'col'), 'row'), may hold values from -0.1875 to 0.1875
- key_first: float32 [1024, 1024], P(('dp', 'col'), 'row'), may hold values from -4 to 4
- key_second: float32 [1024, 1024], P(('dp', 'col'), 'row'), may hold values from 4.847616 to 77.56186
- value_weight: float32 [1024, 1024], P(('dp', 'col'), 'row'), may hold values from -0.1875 to 0.1875
- value_first: float32 [1024, 1024], P(('dp', 'col'), 'row'), may hold values from -32 to 32
- value_second: float32 [1024, 1024], P(('dp', 'col'), 'row'), may hold values from 53.8624 to 861.7984
- output_weight: float32 [1024, 2048], P(('dp', 'col'), 'row'), may hold values from -0.5 to 0.5
- output_first: float32 [1024, 2048], P(('dp', 'col'), 'row'), may hold values from -4 to 4
- output_second: float32 [1024, 2048], P(('dp', 'col'), 'row'), may hold values from 4.847616 to 77.56186
- gate_weight: float32 [1024, 3072], P('row', ('dp', 'col')), may hold values from -0.1875 to 0.1875
- gate_first: float32 [1024, 3072], P('row', ('dp', 'col')), may hold values from -10 to 10
- gate_second: float32 [1024, 3072], P('row', ('dp', 'col')), may hold values from 6.598144 to 105.570305
- up_weight: float32 [1024, 3072], P('row', ('dp', 'col')), may hold values from -0.1875 to 0.1875
- up_first: float32 [1024, 3072], P('row', ('dp', 'col')), may hold values from -10 to 10
- up_second: float32 [1024, 3072], P('row', ('dp', 'col')), may hold values from 6.598144 to 105.570305
- down_weight: float32 [1024, 3072], P('row', ('dp', 'col')), may hold values from -0.109375 to 0.109375
- down_first: float32 [1024, 3072], P('row', ('dp', 'col')), may hold values from -16 to 16
- down_second: float32 [1024, 3072], P('row', ('dp', 'col')), may hold values from 19.390465 to 310.24744
Outputs:
- act_out: bfloat16 [2048, 1024], P(('dp', 'col'), 'row')
- act_grad: float32 [2048, 1024], P(('dp', 'col'), 'row')
- gains_new: float32 [2304], replicated
- gains_first_new: float32 [2304], replicated
- gains_second_new: float32 [2304], replicated
- query_new: float32 [1024, 2048], P(('dp', 'col'), 'row')
- query_first_new: float32 [1024, 2048], P(('dp', 'col'), 'row')
- query_second_new: float32 [1024, 2048], P(('dp', 'col'), 'row')
- key_new: float32 [1024, 1024], P(('dp', 'col'), 'row')
- key_first_new: float32 [1024, 1024], P(('dp', 'col'), 'row')
- key_second_new: float32 [1024, 1024], P(('dp', 'col'), 'row')
- value_new: float32 [1024, 1024], P(('dp', 'col'), 'row')
- value_first_new: float32 [1024, 1024], P(('dp', 'col'), 'row')
- value_second_new: float32 [1024, 1024], P(('dp', 'col'), 'row')
- output_new: float32 [1024, 2048], P(('dp', 'col'), 'row')
- output_first_new: float32 [1024, 2048], P(('dp', 'col'), 'row')
- output_second_new: float32 [1024, 2048], P(('dp', 'col'), 'row')
- gate_new: float32 [1024, 3072], P('row', ('dp', 'col'))
- gate_first_new: float32 [1024, 3072], P('row', ('dp', 'col'))
- gate_second_new: float32 [1024, 3072], P('row', ('dp', 'col'))
- up_new: float32 [1024, 3072], P('row', ('dp', 'col'))
- up_first_new: float32 [1024, 3072], P('row', ('dp', 'col'))
- up_second_new: float32 [1024, 3072], P('row', ('dp', 'col'))
- down_new: float32 [1024, 3072], P('row', ('dp', 'col'))
- down_first_new: float32 [1024, 3072], P('row', ('dp', 'col'))
- down_second_new: float32 [1024, 3072], P('row', ('dp', 'col'))
The draws below stay inside these ranges and needn't reach their ends.
Inputs may be any that keep to these rules, and one draw needn't show every extreme that they name: `segments`: within each sequence of 256 tokens the segment numbers start at 0, never fall, and a document holds at least 32 tokens (the last of a sequence may be cut). Within a segment the positions rise by one from token to token.
All inputs are finite; a program needn't handle non-finite values.
Results may differ from the reference program's by a relative error of at most 0.013.
The reference program's roundings to bfloat16 on the way count: a program that leaves them out, or rounds other values in their place, can miss the bound.
Values may be sent and summed in bfloat16 or wider, within the bound.
No kernel may reach another device: no remote copies, remote signals or barrier semaphores. Data moves between devices by JAX's collectives and lax.ppermute only.
A program may use at most 128 MiB of HBM per device.

```python
import math
import jax
import jax.numpy as jnp
from jax import lax

D = 1024
H = 16
KV = 8
HD = 128
FF = 3072
SEQ_LEN = 256
STEP = 10
QW = 2048
KW = 1024
TOKENS = 2048
N_DP = 2
N_COL = 4


def document_plan(key):
    sequences = TOKENS // SEQ_LEN
    pieces = 16
    lengths = jax.random.randint(key, (sequences, pieces), max(1, SEQ_LEN // 8), SEQ_LEN // 2 + 1)
    lengths = lengths.at[0, :8].set(SEQ_LEN // 8)
    lengths = lengths.at[sequences - 1, 0].set(SEQ_LEN // 2)
    ends = jnp.cumsum(lengths, axis=1)
    begins = ends - lengths
    index = jnp.arange(SEQ_LEN)
    numbers = jnp.sum((ends[:, None, :] <= index[None, :, None]).astype(jnp.int32), axis=2)
    return (begins, numbers)


def draw_segments(key, part):
    begins, numbers = document_plan(key)
    return numbers.reshape(-1).astype(jnp.int32)


def draw_positions(key, part):
    begins, numbers = document_plan(key)
    key = jax.random.fold_in(key, 5)
    starts = jax.random.randint(key, begins.shape, 0, SEQ_LEN)
    starts = starts.at[0, 0].set(0)
    starts = starts.at[begins.shape[0] - 1, 0].set(SEQ_LEN - 1)
    onehot = (numbers[:, :, None] == jnp.arange(begins.shape[1])[None, None, :]).astype(jnp.int32)
    begin_at = jnp.sum(onehot * begins[:, None, :], axis=2)
    start_at = jnp.sum(onehot * starts[:, None, :], axis=2)
    index = jnp.arange(SEQ_LEN)[None, :]
    return (start_at + index - begin_at).reshape(-1).astype(jnp.int32)


def draw_act_in(key, part):
    key = jax.random.fold_in(key, 7)
    along = jnp.arange(D, dtype=jnp.float32) / (D - 1)
    noise = jnp.clip(jax.random.normal(key, (TOKENS, D), jnp.float32), -4.0, 4.0)
    ramp = 0.6 + 1.2 * along
    return (noise * ramp[None, :]).astype(jnp.bfloat16)


def levels(key, shape, split, low, top_value):
    level, own = 1.0, jax.random.fold_in(key, 6)
    for axis_at, shards_of in split:
        heights = jnp.exp(jax.random.uniform(jax.random.fold_in(own, axis_at), (shards_of,), jnp.float32, low / len(split), top_value / len(split)))
        level = level * jnp.repeat(heights, shape[axis_at] // shards_of).reshape([-1 if axis == axis_at else 1 for axis in range(len(shape))])
    return level


def centred(key, shape, scale, reach, shards=(), kind=jnp.bfloat16):
    entries = scale * jax.random.normal(key, shape, jnp.float32)
    if shards:
        entries = entries * levels(key, shape, shards, -0.22, 0.18)
    return jnp.clip(entries, -reach, reach).astype(kind)


def setup_inputs(seed: int = 0) -> dict:
    arg_keys = jax.random.split(jax.random.key(seed), 29)
    act_in = draw_act_in(jax.random.fold_in(arg_keys[28], 71), 0)
    act_cot = centred(arg_keys[1], (TOKENS, D), 1.0, 6.0, ((0, 8), (1, 4)))
    segments = draw_segments(jax.random.fold_in(arg_keys[28], 71), 0)
    positions = draw_positions(jax.random.fold_in(arg_keys[28], 71), 0)
    gains = jnp.clip(1.0 + 0.1 * jax.random.normal(arg_keys[4], (2 * D + 2 * HD,), jnp.float32), 0.5, 1.5)
    gains_first = centred(arg_keys[5], (2 * D + 2 * HD,), (0.111 * TOKENS ** 0.5), 32.0, (), jnp.float32)
    gains_second = jnp.clip(jnp.exp(jax.random.uniform(arg_keys[6], (2 * D + 2 * HD,), jnp.float32, math.log(53.8624), math.log(861.7984))), 53.8624, 861.7984)
    query_weight = centred(arg_keys[7], (D, QW), D ** -0.5, 0.1875, ((0, 8), (1, 4)), jnp.float32)
    query_first = centred(arg_keys[8], (D, QW), (0.111 * 0.3 * TOKENS ** 0.5), 4.0, ((0, 8), (1, 4)), jnp.float32)
    query_second = jnp.clip(jnp.exp(math.log(77.56186) - 2.7725887 * jax.random.uniform(arg_keys[9], (D, QW), jnp.float32) ** levels(arg_keys[9], (D, QW), ((0, 8), (1, 4)), -0.2, 0.2)), 4.847616, 77.56186)
    key_weight = centred(arg_keys[10], (D, KW), D ** -0.5, 0.1875, ((0, 8), (1, 4)), jnp.float32)
    key_first = centred(arg_keys[11], (D, KW), (0.111 * 0.3 * TOKENS ** 0.5), 4.0, ((0, 8), (1, 4)), jnp.float32)
    key_second = jnp.clip(jnp.exp(math.log(77.56186) - 2.7725887 * jax.random.uniform(arg_keys[12], (D, KW), jnp.float32) ** levels(arg_keys[12], (D, KW), ((0, 8), (1, 4)), -0.2, 0.2)), 4.847616, 77.56186)
    value_weight = centred(arg_keys[13], (D, KW), D ** -0.5, 0.1875, ((0, 8), (1, 4)), jnp.float32)
    value_first = centred(arg_keys[14], (D, KW), (0.111 * TOKENS ** 0.5), 32.0, ((0, 8), (1, 4)), jnp.float32)
    value_second = jnp.clip(jnp.exp(math.log(861.7984) - 2.7725887 * jax.random.uniform(arg_keys[15], (D, KW), jnp.float32) ** levels(arg_keys[15], (D, KW), ((0, 8), (1, 4)), -0.2, 0.2)), 53.8624, 861.7984)
    output_weight = centred(arg_keys[16], (D, QW), (QW // 16) ** -0.5, 0.5, ((0, 8), (1, 4)), jnp.float32)
    output_first = centred(arg_keys[17], (D, QW), (0.111 * 0.3 * TOKENS ** 0.5), 4.0, ((0, 8), (1, 4)), jnp.float32)
    output_second = jnp.clip(jnp.exp(math.log(77.56186) - 2.7725887 * jax.random.uniform(arg_keys[18], (D, QW), jnp.float32) ** levels(arg_keys[18], (D, QW), ((0, 8), (1, 4)), -0.2, 0.2)), 4.847616, 77.56186)
    gate_weight = centred(arg_keys[19], (D, FF), D ** -0.5, 0.1875, ((0, 4), (1, 8)), jnp.float32)
    gate_first = centred(arg_keys[20], (D, FF), (0.111 * 0.35 * TOKENS ** 0.5), 10.0, ((0, 4), (1, 8)), jnp.float32)
    gate_second = jnp.clip(jnp.exp(math.log(105.570305) - 2.7725887 * jax.random.uniform(arg_keys[21], (D, FF), jnp.float32) ** levels(arg_keys[21], (D, FF), ((0, 4), (1, 8)), -0.2, 0.2)), 6.598144, 105.570305)
    up_weight = centred(arg_keys[22], (D, FF), D ** -0.5, 0.1875, ((0, 4), (1, 8)), jnp.float32)
    up_first = centred(arg_keys[23], (D, FF), (0.111 * 0.35 * TOKENS ** 0.5), 10.0, ((0, 4), (1, 8)), jnp.float32)
    up_second = jnp.clip(jnp.exp(math.log(105.570305) - 2.7725887 * jax.random.uniform(arg_keys[24], (D, FF), jnp.float32) ** levels(arg_keys[24], (D, FF), ((0, 4), (1, 8)), -0.2, 0.2)), 6.598144, 105.570305)
    down_weight = centred(arg_keys[25], (D, FF), FF ** -0.5, 0.109375, ((0, 4), (1, 8)), jnp.float32)
    down_first = centred(arg_keys[26], (D, FF), (0.111 * 0.6 * TOKENS ** 0.5), 16.0, ((0, 4), (1, 8)), jnp.float32)
    down_second = jnp.clip(jnp.exp(math.log(310.24744) - 2.7725887 * jax.random.uniform(arg_keys[27], (D, FF), jnp.float32) ** levels(arg_keys[27], (D, FF), ((0, 4), (1, 8)), -0.2, 0.2)), 19.390465, 310.24744)
    return dict(act_in=act_in, act_cot=act_cot, segments=segments, positions=positions, gains=gains, gains_first=gains_first, gains_second=gains_second, query_weight=query_weight, query_first=query_first, query_second=query_second, key_weight=key_weight, key_first=key_first, key_second=key_second, value_weight=value_weight, value_first=value_first, value_second=value_second, output_weight=output_weight, output_first=output_first, output_second=output_second, gate_weight=gate_weight, gate_first=gate_first, gate_second=gate_second, up_weight=up_weight, up_first=up_first, up_second=up_second, down_weight=down_weight, down_first=down_first, down_second=down_second)


EPSILON = 1e-06
THETA_BASE = 1000000.0
BETA_FIRST = 0.9
BETA_SECOND = 0.95
ADAM_EPSILON = 1e-08
MATRIX_RATE = 0.04
MATRIX_DECAY = 0.1
GAIN_RATE = 0.5
MASK_VALUE = -1e+30
HIGHEST = lax.Precision.HIGHEST

@jax.custom_vjp
def low(v):
    return lax.optimization_barrier(v.astype(jnp.bfloat16)).astype(jnp.float32)

@jax.custom_vjp
def low_back(v):
    return v

def low_keep(v):
    return (low(v), None)

def low_pass(kept, grad):
    return (grad,)

def back_keep(v):
    return (v, None)

def back_low(kept, grad):
    return (low(grad),)
low.defvjp(low_keep, low_pass)
low_back.defvjp(back_keep, back_low)

def matmul(left, right):
    return jnp.dot(left, right, precision=HIGHEST)

def rotary_tables(positions):
    half = HD // 2
    inverse = THETA_BASE ** (-(jnp.arange(half, dtype=jnp.float32) * 2.0 / HD))
    angle = positions.astype(jnp.float32)[..., None] * inverse
    return (jnp.cos(angle), jnp.sin(angle))

def rotate(values, cosine, sine):
    half = values.shape[-1] // 2
    first = values[..., :half]
    second = values[..., half:]
    cosine = cosine[..., None, :]
    sine = sine[..., None, :]
    return jnp.concatenate([first * cosine - second * sine, second * cosine + first * sine], axis=-1)

def head_norm(values, gain):
    return values * lax.rsqrt(lax.optimization_barrier(jnp.mean(values * values, axis=-1, keepdims=True)) + EPSILON) * gain

def attend(item):
    queries, keys, values, segments = item
    length = queries.shape[0]
    grouped = queries.reshape(length, KV, H // KV, HD)
    scores = jnp.einsum('qgmd,kgd->gmqk', grouped, keys, precision=HIGHEST) * HD ** (-0.5)
    scores = low_back(scores)
    index = jnp.arange(length)
    allowed = (segments[:, None] == segments[None, :]) & (index[None, :] <= index[:, None])
    scores = jnp.where(allowed, scores, MASK_VALUE)
    probs = low(jax.nn.softmax(scores, axis=-1))
    context = jnp.einsum('gmqk,kgd->qgmd', probs, values, precision=HIGHEST)
    return context.reshape(length, H * HD)

def layer(inputs, segments, positions, query_matrix, key_matrix, value_matrix, output_matrix, gate_matrix, up_matrix, down_matrix, gains):
    count = inputs.shape[0]
    length = inputs.shape[1]
    gain_in = gains[:D]
    gain_mid = gains[D:2 * D]
    gain_query = gains[2 * D:2 * D + HD]
    gain_key = gains[2 * D + HD:]
    scale_in = lax.rsqrt(lax.optimization_barrier(jnp.mean(inputs * inputs, axis=-1, keepdims=True)) + EPSILON)
    normed = low(inputs * scale_in * gain_in).reshape(-1, D)
    queries = low_back(matmul(normed, query_matrix)).reshape(count, length, H, HD)
    keys = low_back(matmul(normed, key_matrix)).reshape(count, length, KV, HD)
    values = low(low_back(matmul(normed, value_matrix))).reshape(count, length, KV, HD)
    queries = head_norm(queries, gain_query)
    keys = head_norm(keys, gain_key)
    cosine, sine = rotary_tables(positions)
    queries = low(rotate(queries, cosine, sine))
    keys = low(rotate(keys, cosine, sine))
    context = lax.map(jax.checkpoint(attend), (queries, keys, values, segments))
    context = low(low_back(context)).reshape(-1, H * HD)
    branch = low_back(matmul(context, output_matrix.T)).reshape(count, length, D)
    resid = inputs + branch
    scale_mid = lax.rsqrt(lax.optimization_barrier(jnp.mean(resid * resid, axis=-1, keepdims=True)) + EPSILON)
    mid = low(resid * scale_mid * gain_mid).reshape(-1, D)
    gate = low_back(matmul(mid, gate_matrix))
    upward = low_back(matmul(mid, up_matrix))
    hidden = low(jax.nn.silu(gate) * upward)
    down = low_back(matmul(hidden, down_matrix.T)).reshape(count, length, D)
    return resid + down

def adamw(weight, first, second, grad, rate, decay):
    first_new = BETA_FIRST * first + (1.0 - BETA_FIRST) * grad
    second_new = BETA_SECOND * second + (1.0 - BETA_SECOND) * grad * grad
    first_hat = first_new / (1.0 - BETA_FIRST ** STEP)
    second_hat = second_new / (1.0 - BETA_SECOND ** STEP)
    weight_new = weight - rate * (first_hat / (jnp.sqrt(second_hat) + ADAM_EPSILON) + decay * weight)
    return (weight_new, first_new, second_new)

def reference(act_in, act_cot, segments, positions, gains, gains_first, gains_second, query_weight, query_first, query_second, key_weight, key_first, key_second, value_weight, value_first, value_second, output_weight, output_first, output_second, gate_weight, gate_first, gate_second, up_weight, up_first, up_second, down_weight, down_first, down_second):
    sequences = N_DP * N_COL
    group = min(sequences, max(1, 4096 // SEQ_LEN))
    count = sequences // group
    params = (low(query_weight), low(key_weight), low(value_weight), low(output_weight), low(gate_weight), low(up_weight), low(down_weight), gains)
    inputs = act_in.astype(jnp.float32).reshape(count, group, SEQ_LEN, D)
    cotangents = act_cot.astype(jnp.float32).reshape(count, group, SEQ_LEN, D)
    segment_rows = segments.reshape(count, group, SEQ_LEN)
    position_rows = positions.reshape(count, group, SEQ_LEN)

    def one_group(totals, item):
        block_in, block_cot, block_seg, block_pos = item

        def forward(values, *weights):
            return layer(values, block_seg, block_pos, *weights)
        output, pullback = jax.vjp(forward, block_in, *params)
        grads = pullback(block_cot)
        totals = tuple((total + grad for total, grad in zip(totals, grads[1:])))
        return (totals, (output.astype(jnp.bfloat16), grads[0]))
    zeros = tuple((jnp.zeros_like(matrix) for matrix in params))
    totals, (outputs, input_grads) = lax.scan(one_group, zeros, (inputs, cotangents, segment_rows, position_rows))
    query_grad, key_grad, value_grad, output_grad, gate_grad, up_grad, down_grad, gains_grad = totals
    gains_new, gains_first_new, gains_second_new = adamw(gains, gains_first, gains_second, gains_grad, GAIN_RATE, 0.0)
    query_new, query_first_new, query_second_new = adamw(query_weight, query_first, query_second, query_grad, MATRIX_RATE, MATRIX_DECAY)
    key_new, key_first_new, key_second_new = adamw(key_weight, key_first, key_second, key_grad, MATRIX_RATE, MATRIX_DECAY)
    value_new, value_first_new, value_second_new = adamw(value_weight, value_first, value_second, value_grad, MATRIX_RATE, MATRIX_DECAY)
    output_new, output_first_new, output_second_new = adamw(output_weight, output_first, output_second, output_grad, MATRIX_RATE, MATRIX_DECAY)
    gate_new, gate_first_new, gate_second_new = adamw(gate_weight, gate_first, gate_second, gate_grad, MATRIX_RATE, MATRIX_DECAY)
    up_new, up_first_new, up_second_new = adamw(up_weight, up_first, up_second, up_grad, MATRIX_RATE, MATRIX_DECAY)
    down_new, down_first_new, down_second_new = adamw(down_weight, down_first, down_second, down_grad, MATRIX_RATE, MATRIX_DECAY)
    return (outputs.reshape(TOKENS, D), input_grads.reshape(TOKENS, D), gains_new, gains_first_new, gains_second_new, query_new, query_first_new, query_second_new, key_new, key_first_new, key_second_new, value_new, value_first_new, value_second_new, output_new, output_first_new, output_second_new, gate_new, gate_first_new, gate_second_new, up_new, up_first_new, up_second_new, down_new, down_first_new, down_second_new)
```

```python
import functools

import jax
import jax.numpy as jnp
from jax import lax
from jax.experimental import pallas as pl
from jax.experimental.pallas import tpu as pltpu
from jax.sharding import PartitionSpec as P

D = 1024
HD = 128
STEP = 10

EPSILON = 1e-06
THETA_BASE = 1000000.0
BETA_FIRST = 0.9
BETA_SECOND = 0.95
ADAM_EPSILON = 1e-08
MATRIX_RATE = 0.04
MATRIX_DECAY = 0.1
GAIN_RATE = 0.5
MASK_VALUE = -1e30
LANE = 128
BLOCKS = D // LANE
PLANE = ("dp", "col")
F32 = jnp.float32
BF16 = jnp.bfloat16


def mm(left, right):
    return jnp.dot(left, right, preferred_element_type=F32)


def mm_nt(left, right):
    return lax.dot_general(left, right, (((1,), (1,)), ((), ())), preferred_element_type=F32)


def mm_tn(left, right):
    return lax.dot_general(left, right, (((0,), (0,)), ((), ())), preferred_element_type=F32)


def lanes(block):
    return pl.ds(pl.multiple_of(block * LANE, LANE), LANE)


def rows_of(block, size):
    return pl.ds(pl.multiple_of(block * size, size), size)


def call(kernel, outs, *args, scalars=0, scratch=(), flops=1e8, limit=32):
    vmem = pl.BlockSpec(memory_space=pltpu.VMEM)
    smem = pl.BlockSpec(memory_space=pltpu.SMEM)
    moved = sum(a.size * a.dtype.itemsize for a in list(args) + list(outs))
    return pl.pallas_call(
        kernel,
        out_shape=list(outs),
        in_specs=[smem] * scalars + [vmem] * (len(args) - scalars),
        out_specs=[vmem] * len(outs),
        scratch_shapes=list(scratch),
        compiler_params=pltpu.CompilerParams(vmem_limit_bytes=limit << 20),
        cost_estimate=pl.CostEstimate(flops=int(flops), bytes_accessed=int(moved), transcendentals=0),
    )(*args)


def shape(dims, dtype):
    return jax.ShapeDtypeStruct(tuple(dims), dtype)


def attend_kernel(place, x_ref, wz_ref, wo_ref, g1_ref, gq_ref, gk_ref, cos_ref, sin_ref, segc_ref, segr_ref,
                  ctx_ref, prob_ref, q_ref, k_ref, v_ref, raw_ref, norm_ref):
    z = place[0]
    x = x_ref[...].astype(F32)
    r1 = lax.rsqrt(jnp.mean(x * x, axis=-1, keepdims=True) + EPSILON)
    for j in range(BLOCKS):
        b = place[1 + j]
        block = x_ref[:, lanes(b ^ (2 * z))].astype(F32)
        norm_ref[:, j * LANE:(j + 1) * LANE] = (block * r1 * g1_ref[:, lanes(b)]).astype(BF16)
    half = D // 2
    qkv = mm(norm_ref[:, :half], wz_ref[...]) + mm(norm_ref[:, half:], wo_ref[...])
    qw, kw = q_ref.shape[1], k_ref.shape[1]
    raw_ref[...] = qkv[:, :qw + kw]
    v_ref[...] = qkv[:, qw + kw:].astype(BF16)
    cosine, sine = cos_ref[...], sin_ref[...]
    for h in range((qw + kw) // HD):
        part = qkv[:, h * HD:(h + 1) * HD]
        is_q = h * HD < qw
        gain = gq_ref[...] if is_q else gk_ref[...]
        part = part * lax.rsqrt(jnp.mean(part * part, axis=-1, keepdims=True) + EPSILON) * gain
        part = (part * cosine + pltpu.roll(part, HD // 2, 1) * sine).astype(BF16)
        if is_q:
            q_ref[:, h * HD:(h + 1) * HD] = part
        else:
            at = h * HD - qw
            k_ref[:, at:at + HD] = part
    length = x.shape[0]
    i = lax.broadcasted_iota(jnp.int32, (length, length), 0)
    j = lax.broadcasted_iota(jnp.int32, (length, length), 1)
    allowed = (segc_ref[...] == segr_ref[...]) & (j <= i)
    heads, groups = qw // HD, kw // HD
    for h in range(heads):
        g = h * groups // heads
        s = mm_nt(q_ref[:, h * HD:(h + 1) * HD], k_ref[:, g * HD:(g + 1) * HD]) * HD ** (-0.5)
        s = jnp.where(allowed, s, MASK_VALUE)
        peak = jnp.max(s, axis=-1, keepdims=True)
        total = peak + jnp.log(jnp.sum(jnp.exp(s - peak), axis=-1, keepdims=True))
        p = jnp.exp(s - total)
        prob_ref[h * length:(h + 1) * length, :] = p
        ctx_ref[:, h * HD:(h + 1) * HD] = mm(p.astype(BF16), v_ref[:, g * HD:(g + 1) * HD]).astype(BF16)


def branch_kernel(place, ctx_ref, oz_ref, oo_ref, own_ref, *rest):
    sends, scratch = rest[:-1], rest[-1]
    z = place[0]
    half = D // 2
    ctx = ctx_ref[...]
    scratch[:, :half] = mm_nt(ctx, oz_ref[...])
    scratch[:, half:] = mm_nt(ctx, oo_ref[...])
    size = own_ref.shape[0]
    for k, out in enumerate((own_ref,) + sends):
        to = z ^ k
        for j in range(BLOCKS):
            b = place[1 + j]
            out[:, lanes(b ^ (2 * to))] = scratch[rows_of(to, size), j * LANE:(j + 1) * LANE].astype(out.dtype)


def mid_kernel(n, place, x_ref, g2_ref, *rest):
    terms, (resid_ref, mid_ref) = rest[:n], rest[n:]
    z = place[0]
    size = resid_ref.shape[0]
    resid = x_ref[rows_of(z, size), :].astype(F32)
    total = terms[0][...].astype(F32)
    for term in terms[1:]:
        total = total + term[...].astype(F32)
    resid = resid + total
    resid_ref[...] = resid
    scale = lax.rsqrt(jnp.mean(resid * resid, axis=-1, keepdims=True) + EPSILON)
    for j in range(BLOCKS):
        at = slice(j * LANE, (j + 1) * LANE)
        mid_ref[:, at] = (resid[:, at] * scale * g2_ref[:, lanes(j ^ (2 * z))]).astype(BF16)


def units_math(gate, up, dhidden):
    sigmoid = jax.nn.sigmoid(gate)
    hidden = (gate * sigmoid * up).astype(BF16)
    dgate = (dhidden * up * sigmoid * (1.0 + gate * (1.0 - sigmoid))).astype(BF16)
    dup = (dhidden * gate * sigmoid).astype(BF16)
    return hidden, dgate, dup


def units_kernel(n, mz_ref, mo_ref, cz_ref, co_ref, *rest):
    w = rest[:n]
    dz_ref, do_ref, az_ref, ao_ref, hid_ref, dgu_ref = rest[n:]
    units = w[0].shape[1] // 3
    part = w[0].shape[0]
    tokens = mz_ref.shape[0]
    for t, (m_ref, c_ref, d_ref, a_ref) in enumerate(
            ((mz_ref, cz_ref, dz_ref, az_ref), (mo_ref, co_ref, do_ref, ao_ref))):
        at = slice(t * tokens, (t + 1) * tokens)
        gu = dh = None
        for k in range(n):
            fs = slice(k * part, (k + 1) * part)
            g_k = mm(m_ref[:, fs], w[k][:, :2 * units])
            h_k = mm(c_ref[:, fs], w[k][:, 2 * units:])
            gu = g_k if gu is None else gu + g_k
            dh = h_k if dh is None else dh + h_k
        hidden, dgate, dup = units_math(gu[:, :units], gu[:, units:], dh)
        hid_ref[at, :] = hidden
        dgu_ref[at, :units] = dgate
        dgu_ref[at, units:] = dup
    for t, (d_ref, a_ref) in enumerate(((dz_ref, az_ref), (do_ref, ao_ref))):
        at = slice(t * tokens, (t + 1) * tokens)
        for k in range(n):
            fs = slice(k * part, (k + 1) * part)
            d_ref[:, fs] = mm_nt(dgu_ref[at, :], w[k][:, :2 * units]).astype(d_ref.dtype)
            a_ref[:, fs] = mm_nt(hid_ref[at, :], w[k][:, 2 * units:]).astype(a_ref.dtype)


def units_grad_kernel(n, mz_ref, mo_ref, cz_ref, co_ref, hid_ref, dgu_ref, *outs):
    units = hid_ref.shape[1]
    part = outs[0].shape[0]
    tokens = mz_ref.shape[0]
    for k in range(n):
        fs = slice(k * part, (k + 1) * part)
        out = outs[k]
        out[:, :2 * units] = (
            mm_tn(mz_ref[:, fs], dgu_ref[:tokens, :]) + mm_tn(mo_ref[:, fs], dgu_ref[tokens:, :])
        ).astype(out.dtype)
        out[:, 2 * units:] = (
            mm_tn(cz_ref[:, fs], hid_ref[:tokens, :]) + mm_tn(co_ref[:, fs], hid_ref[tokens:, :])
        ).astype(out.dtype)


def mid_back_kernel(n, place, resid_ref, cot_ref, g2_ref, *rest):
    terms, (grad_ref, gain_ref) = rest[:n], rest[n:]
    z = place[0]
    dmid = terms[0][...].astype(F32)
    for term in terms[1:]:
        dmid = dmid + term[...].astype(F32)
    resid = resid_ref[...]
    r2 = lax.rsqrt(jnp.mean(resid * resid, axis=-1, keepdims=True) + EPSILON)
    inner = None
    for j in range(BLOCKS):
        at = slice(j * LANE, (j + 1) * LANE)
        b = j ^ (2 * z)
        part = dmid[:, at] * g2_ref[:, lanes(b)] * resid[:, at]
        inner = part if inner is None else inner + part
        gain_ref[:, lanes(b)] = jnp.sum(dmid[:, at] * resid[:, at] * r2, axis=0, keepdims=True)
    inner = jnp.sum(inner, axis=-1, keepdims=True)
    back = r2 * r2 * r2 * inner / D
    for j in range(BLOCKS):
        at = slice(j * LANE, (j + 1) * LANE)
        grad_ref[:, at] = (
            cot_ref[:, at].astype(F32) + r2 * g2_ref[:, lanes(j ^ (2 * z))] * dmid[:, at] - resid[:, at] * back
        ).astype(BF16)


def output_grad_kernel(n, place, ctx_ref, *rest):
    pieces, (dbr_ref, gz_ref, go_ref) = rest[:n], rest[n:]
    z = place[0]
    size = pieces[0].shape[0]
    for k in range(n):
        frm = z ^ k
        for j in range(BLOCKS):
            b = place[1 + j]
            dbr_ref[rows_of(frm, size), j * LANE:(j + 1) * LANE] = pieces[k][:, lanes(b ^ (2 * frm))]
    half = D // 2
    go_ref[...] = mm_tn(dbr_ref[:, half:], ctx_ref[...]).astype(go_ref.dtype)
    gz_ref[...] = mm_tn(dbr_ref[:, :half], ctx_ref[...]).astype(gz_ref.dtype)


def attend_back_kernel(dbr_ref, oz_ref, oo_ref, prob_ref, q_ref, k_ref, v_ref, raw_ref, gq_ref, gk_ref, cos_ref, sin_ref,
                       dqkv_ref, dgq_ref, dgk_ref):
    half = D // 2
    dctx = (mm(dbr_ref[:, :half], oz_ref[...]) + mm(dbr_ref[:, half:], oo_ref[...])).astype(BF16)
    qw, kw = q_ref.shape[1], k_ref.shape[1]
    heads, groups = qw // HD, kw // HD
    length = dbr_ref.shape[0]
    cosine, sine = cos_ref[...], sin_ref[...]

    def back(grad, h, gain):
        grad = grad * cosine - pltpu.roll(grad, HD // 2, 1) * sine
        value = raw_ref[:, h * HD:(h + 1) * HD]
        factor = lax.rsqrt(jnp.mean(value * value, axis=-1, keepdims=True) + EPSILON)
        inner = jnp.sum(grad * gain * value, axis=-1, keepdims=True)
        out = factor * gain * grad - value * (factor * factor * factor) * inner / HD
        return out.astype(BF16), jnp.sum(grad * value * factor, axis=0, keepdims=True)

    dgq = dgk = None
    for g in range(groups):
        dk = dv = None
        keys = k_ref[:, g * HD:(g + 1) * HD]
        vals = v_ref[:, g * HD:(g + 1) * HD]
        for h in range(g * heads // groups, (g + 1) * heads // groups):
            hs = slice(h * HD, (h + 1) * HD)
            p = prob_ref[h * length:(h + 1) * length, :]
            dp = mm_nt(dctx[:, hs], vals)
            delta = jnp.sum(p * dp, axis=-1, keepdims=True)
            ds = (p * (dp - delta)).astype(BF16)
            dq, gain_part = back(mm(ds, keys) * HD ** (-0.5), h, gq_ref[...])
            dqkv_ref[:, hs] = dq
            dgq = gain_part if dgq is None else dgq + gain_part
            dk_h = mm_tn(ds, q_ref[:, hs])
            dv_h = mm_tn(p.astype(BF16), dctx[:, hs])
            dk = dk_h if dk is None else dk + dk_h
            dv = dv_h if dv is None else dv + dv_h
        dk, gain_part = back(dk * HD ** (-0.5), heads + g, gk_ref[...])
        dgk = gain_part if dgk is None else dgk + gain_part
        dqkv_ref[:, qw + g * HD:qw + (g + 1) * HD] = dk
        dqkv_ref[:, qw + kw + g * HD:qw + kw + (g + 1) * HD] = dv.astype(BF16)
    dgq_ref[...] = dgq
    dgk_ref[...] = dgk


def qkv_grad_kernel(norm_ref, dqkv_ref, gz_ref, go_ref):
    half = D // 2
    go_ref[...] = mm_tn(norm_ref[:, half:], dqkv_ref[...]).astype(go_ref.dtype)
    gz_ref[...] = mm_tn(norm_ref[:, :half], dqkv_ref[...]).astype(gz_ref.dtype)


def input_grad_kernel(n, place, dqkv_ref, wz_ref, wo_ref, x_ref, g1_ref, *rest):
    outs, gain_ref, dn_ref, term_ref = rest[:n], rest[n], rest[n + 1], rest[n + 2]
    z = place[0]
    half = D // 2
    dqkv = dqkv_ref[...]
    dn_ref[:, :half] = mm_nt(dqkv, wz_ref[...])
    dn_ref[:, half:] = mm_nt(dqkv, wo_ref[...])
    x = x_ref[...].astype(F32)
    r1 = lax.rsqrt(jnp.mean(x * x, axis=-1, keepdims=True) + EPSILON)
    inner = None
    for j in range(BLOCKS):
        b = place[1 + j]
        dn = dn_ref[:, j * LANE:(j + 1) * LANE]
        xb = x_ref[:, lanes(b ^ (2 * z))].astype(F32)
        part = dn * g1_ref[:, lanes(b)] * xb
        inner = part if inner is None else inner + part
        gain_ref[:, lanes(b)] = jnp.sum(dn * xb * r1, axis=0, keepdims=True)
    inner = jnp.sum(inner, axis=-1, keepdims=True)
    back = r1 * r1 * r1 * inner / D
    for j in range(BLOCKS):
        b = place[1 + j]
        at = lanes(b ^ (2 * z))
        xb = x_ref[:, at].astype(F32)
        term_ref[:, at] = r1 * g1_ref[:, lanes(b)] * dn_ref[:, j * LANE:(j + 1) * LANE] - xb * back
    width = outs[0].shape[1]
    for k, out in enumerate(outs):
        out[...] = term_ref[:, k * width:(k + 1) * width].astype(out.dtype)


def act_grad_kernel(n, place, *rest):
    pieces, terms, out_ref = rest[:n], rest[n:2 * n], rest[2 * n]
    z = place[0]
    width = out_ref.shape[1]
    size = pieces[0].shape[0]
    for k in range(n):
        at = rows_of(z ^ k, size)
        total = terms[0][at, :].astype(F32)
        for term in terms[1:]:
            total = total + term[at, :].astype(F32)
        out_ref[at, :] = pieces[k][:, k * width:(k + 1) * width].astype(F32) + total


def act_out_kernel(n, resid_ref, *rest):
    terms, outs = rest[:n], rest[n:]
    total = terms[0][...].astype(F32)
    for term in terms[1:]:
        total = total + term[...].astype(F32)
    total = (resid_ref[...] + total).astype(BF16)
    width = outs[0].shape[1]
    for k, out in enumerate(outs):
        out[...] = total[:, k * width:(k + 1) * width]


def place_kernel(n, place, *rest):
    pieces, out_ref = rest[:n], rest[n]
    size = pieces[0].shape[0]
    for k in range(n):
        out_ref[rows_of(place[0] ^ k, size), :] = pieces[k][...]


def adamw(weight, first, second, grad, rate, decay):
    first_new = BETA_FIRST * first + (1.0 - BETA_FIRST) * grad
    second_new = BETA_SECOND * second + (1.0 - BETA_SECOND) * grad * grad
    first_hat = first_new / (1.0 - BETA_FIRST**STEP)
    second_hat = second_new / (1.0 - BETA_SECOND**STEP)
    weight_new = weight - rate * (
        first_hat / (jnp.sqrt(second_hat) + ADAM_EPSILON) + decay * weight
    )
    return (weight_new, first_new, second_new)


def body(sizes, act_in, act_cot, segments, positions, gains, gains_first, gains_second,
         query_weight, query_first, query_second, key_weight, key_first, key_second,
         value_weight, value_first, value_second, output_weight, output_first, output_second,
         gate_weight, gate_first, gate_second, up_weight, up_first, up_second,
         down_weight, down_first, down_second):
    n_dp, n_row, n_col = sizes
    n_plane = n_dp * n_col
    paired = n_dp == 2 and n_col == 4
    z = lax.axis_index("row").astype(jnp.int32)
    p = lax.axis_index(PLANE).astype(jnp.int32)

    def over_row(value, k):
        return lax.ppermute(value, "row", [(i, i ^ k) for i in range(n_row)])

    def over_plane(value, k):
        return lax.ppermute(value, PLANE, [(i, i ^ k) for i in range(n_plane)])

    def gather_row(value):
        return [value] + [over_row(value, k) for k in range(1, n_row)]

    def scatter_row(values):
        return [values[0]] + [over_row(values[k], k) for k in range(1, n_row)]

    def gather_plane(value):
        if not paired:
            whole = lax.all_gather(value, PLANE, axis=0, tiled=True)
            half = whole.shape[0] // 2
            return whole[:half], whole[half:]
        same = jnp.concatenate([value] + [over_plane(value, k) for k in (2, 4, 6)], axis=0)
        return same, over_plane(same, 1)

    def scatter_plane(same, other):
        if not paired:
            whole = jnp.concatenate([same, other.astype(F32)], axis=0)
            return [lax.psum_scatter(whole, PLANE, scatter_dimension=0, tiled=True)]
        total = same + over_plane(other, 1).astype(F32)
        size = total.shape[0] // 4
        return [total[:size]] + [
            over_plane(total[i * size:(i + 1) * size].astype(BF16), k) for i, k in ((1, 2), (2, 4), (3, 6))
        ]

    def sum_all(value):
        if not paired:
            return lax.psum(value, ("dp", "row", "col"))
        value = value + over_plane(value, 1)
        value = value + over_plane(value, 2) + over_plane(value, 4) + over_plane(value, 6)
        return value + over_row(value, 1) + over_row(value, 2) + over_row(value, 3)

    order = jnp.array([0, 2, 4, 6, 1, 3, 5, 7], jnp.int32) ^ p if paired else jnp.arange(BLOCKS, dtype=jnp.int32)
    place = jnp.concatenate([z[None], order])

    w_qkv = jnp.concatenate([query_weight, key_weight, value_weight], axis=1).astype(BF16)
    qkv_z, qkv_o = gather_plane(w_qkv)
    x_row = jnp.concatenate(gather_row(act_in), axis=1)
    out_z, out_o = gather_plane(output_weight.astype(BF16))
    w_units = gather_row(jnp.concatenate([gate_weight, up_weight, down_weight], axis=1).astype(BF16))
    length = act_in.shape[0]
    size = length // n_row
    cot_own = jnp.concatenate(
        scatter_row([lax.dynamic_slice_in_dim(act_cot, (z ^ k) * size, size, 0) for k in range(n_row)]), axis=1)
    cot_z, cot_o = gather_plane(cot_own)

    gain_in = gains[None, :D]
    gain_mid = gains[None, D:2 * D]
    gain_query = gains[None, 2 * D:2 * D + HD]
    gain_key = gains[None, 2 * D + HD:]
    inverse = THETA_BASE ** (-(jnp.arange(HD // 2, dtype=F32) * 2.0 / HD))
    angle = positions.astype(F32)[:, None] * inverse
    cosine, sine = jnp.cos(angle), jnp.sin(angle)
    cosine = jnp.concatenate([cosine, cosine], axis=1)
    sine = jnp.concatenate([-sine, sine], axis=1)

    qw, kw = query_weight.shape[1], key_weight.shape[1]
    heads = qw // HD
    context, probs, queries, keys, values, raw, normed = call(
        attend_kernel,
        [shape((length, qw), BF16), shape((heads * length, length), F32), shape((length, qw), BF16),
         shape((length, kw), BF16), shape((length, kw), BF16), shape((length, qw + kw), F32), shape((length, D), BF16)],
        place, x_row, qkv_z, qkv_o, gain_in, gain_query, gain_key, cosine, sine, segments[:, None], segments[None, :],
        scalars=1, flops=2 * length * D * (qw + 2 * kw) + 4 * heads * length * length * HD)
    terms = call(
        branch_kernel,
        [shape((size, D), F32)] + [shape((size, D), BF16)] * (n_row - 1),
        place, context, out_z, out_o,
        scalars=1, scratch=[pltpu.VMEM((length, D), F32)], flops=2 * length * D * qw)
    terms = scatter_row(terms)
    resid, mid = call(
        functools.partial(mid_kernel, n_row),
        [shape((size, D), F32), shape((size, D), BF16)],
        place, x_row, gain_mid, *terms, scalars=1, flops=1e6)

    mid_z, mid_o = gather_plane(mid)
    units = gate_weight.shape[1]
    tokens = mid_z.shape[0]
    if units % LANE == 0 and tokens <= 512:
        dmid_z, dmid_o, down_z, down_o, hidden, d_units = call(
            functools.partial(units_kernel, n_row),
            [shape((tokens, D), F32), shape((tokens, D), BF16), shape((tokens, D), F32), shape((tokens, D), BF16),
             shape((2 * tokens, units), BF16), shape((2 * tokens, 2 * units), BF16)],
            mid_z, mid_o, cot_z, cot_o, *w_units, flops=2 * 2 * tokens * D * units * 6)
        unit_grads = call(
            functools.partial(units_grad_kernel, n_row),
            [shape((D // n_row, 3 * units), F32 if k == 0 else BF16) for k in range(n_row)],
            mid_z, mid_o, cot_z, cot_o, hidden, d_units, flops=2 * 2 * tokens * D * units * 3)
    else:
        mid_all = jnp.concatenate([mid_z, mid_o], axis=0)
        cot_all = jnp.concatenate([cot_z, cot_o], axis=0)
        joined = jnp.concatenate(w_units, axis=0)
        gate_up = mm(mid_all, joined[:, :2 * units])
        hidden, dgate, dup = units_math(gate_up[:, :units], gate_up[:, units:], mm(cot_all, joined[:, 2 * units:]))
        d_units = jnp.concatenate([dgate, dup], axis=1)
        dmid = mm_nt(d_units, joined[:, :2 * units])
        down = mm_nt(hidden, joined[:, 2 * units:])
        dmid_z, dmid_o, down_z, down_o = dmid[:tokens], dmid[tokens:], down[:tokens], down[tokens:]
        whole = jnp.concatenate([mm_tn(mid_all, d_units), mm_tn(cot_all, hidden)], axis=1)
        unit_grads = [
            part.astype(F32 if k == 0 else BF16) for k, part in enumerate(jnp.split(whole, n_row, axis=0))
        ]
    dmid_terms = scatter_plane(dmid_z, dmid_o)
    branch_grad, mid_gain_grad = call(
        functools.partial(mid_back_kernel, len(dmid_terms)),
        [shape((size, D), BF16), shape((1, D), F32)],
        place, resid, cot_own, gain_mid, *dmid_terms, scalars=1, flops=1e6)

    pieces = gather_row(branch_grad)
    unit_grads = scatter_row(unit_grads)
    down_terms = scatter_plane(down_z, down_o)
    dbranch, out_grad_z, out_grad_o = call(
        functools.partial(output_grad_kernel, n_row),
        [shape((length, D), BF16), shape((D // 2, qw), F32), shape((D // 2, qw), BF16)],
        place, context, *pieces, scalars=1, flops=2 * length * D * qw)
    out_terms = scatter_plane(out_grad_z, out_grad_o)
    dqkv, query_gain_grad, key_gain_grad = call(
        attend_back_kernel,
        [shape((length, qw + 2 * kw), BF16), shape((1, HD), F32), shape((1, HD), F32)],
        dbranch, out_z, out_o, probs, queries, keys, values, raw, gain_query, gain_key, cosine, sine,
        flops=2 * length * D * qw + 8 * heads * length * length * HD)
    qkv_grad_z, qkv_grad_o = call(
        qkv_grad_kernel,
        [shape((D // 2, qw + 2 * kw), F32), shape((D // 2, qw + 2 * kw), BF16)],
        normed, dqkv, flops=2 * length * D * (qw + 2 * kw))
    qkv_terms = scatter_plane(qkv_grad_z, qkv_grad_o)
    width = act_in.shape[1]
    *in_terms, in_gain_grad = call(
        functools.partial(input_grad_kernel, n_row),
        [shape((length, width), F32 if k == 0 else BF16) for k in range(n_row)] + [shape((1, D), F32)],
        place, dqkv, qkv_z, qkv_o, x_row, gain_in,
        scalars=1, scratch=[pltpu.VMEM((length, D), F32)] * 2, flops=2 * length * D * (qw + 2 * kw))
    in_terms = scatter_row(in_terms)
    gains_grad = sum_all(jnp.concatenate([in_gain_grad, mid_gain_grad, query_gain_grad, key_gain_grad], axis=1))[0]

    out_parts = call(
        functools.partial(act_out_kernel, len(down_terms)),
        [shape((size, width), BF16)] * n_row,
        resid, *down_terms, flops=1e6)
    out_parts = scatter_row(out_parts)
    (act_out,) = call(functools.partial(place_kernel, n_row), [shape((length, width), BF16)],
                      place, *out_parts, scalars=1, flops=1e6)
    (act_grad,) = call(functools.partial(act_grad_kernel, n_row), [shape((length, width), F32)],
                       place, *pieces, *in_terms, scalars=1, flops=1e6)

    def total(terms):
        out = terms[0].astype(F32)
        for term in terms[1:]:
            out = out + term.astype(F32)
        return out

    unit_total, out_total, qkv_total = total(unit_grads), total(out_terms), total(qkv_terms)
    matrix = functools.partial(adamw, rate=MATRIX_RATE, decay=MATRIX_DECAY)
    return (
        act_out,
        act_grad,
        *adamw(gains, gains_first, gains_second, gains_grad, GAIN_RATE, 0.0),
        *matrix(query_weight, query_first, query_second, qkv_total[:, :qw]),
        *matrix(key_weight, key_first, key_second, qkv_total[:, qw:qw + kw]),
        *matrix(value_weight, value_first, value_second, qkv_total[:, qw + kw:]),
        *matrix(output_weight, output_first, output_second, out_total),
        *matrix(gate_weight, gate_first, gate_second, unit_total[:, :units]),
        *matrix(up_weight, up_first, up_second, unit_total[:, units:2 * units]),
        *matrix(down_weight, down_first, down_second, unit_total[:, 2 * units:]),
    )


def solution(mesh):
    token, proj, unit = P(PLANE, "row"), P(PLANE, "row"), P("row", PLANE)
    sizes = (mesh.shape["dp"], mesh.shape["row"], mesh.shape["col"])
    return jax.shard_map(
        functools.partial(body, sizes),
        mesh=mesh,
        in_specs=(token, token, P(PLANE), P(PLANE)) + (P(),) * 3 + (proj,) * 12 + (unit,) * 9,
        out_specs=(token, token) + (P(),) * 3 + (proj,) * 12 + (unit,) * 9,
        check_vma=False,
    )
```

```python
import functools
import math

import jax
import jax.numpy as jnp
from jax import lax
from jax.experimental import pallas as pl
from jax.experimental.pallas import tpu as pltpu
from jax.sharding import PartitionSpec as P

D = 1024
HD = 128
STEP = 10

EPSILON = 1e-06
THETA_BASE = 1000000.0
BETA_FIRST = 0.9
BETA_SECOND = 0.95
ADAM_EPSILON = 1e-08
MATRIX_RATE = 0.04
MATRIX_DECAY = 0.1
GAIN_RATE = 0.5
MASK_VALUE = -1e30
LANE = 128
BLOCKS = D // LANE
PLANE = ("dp", "col")
F32 = jnp.float32
BF16 = jnp.bfloat16


def mm(left, right):
    return jnp.dot(left, right, preferred_element_type=F32)


def mm_nt(left, right):
    return lax.dot_general(left, right, (((1,), (1,)), ((), ())), preferred_element_type=F32)


def mm_tn(left, right):
    return lax.dot_general(left, right, (((0,), (0,)), ((), ())), preferred_element_type=F32)


def lanes(block):
    return pl.ds(pl.multiple_of(block * LANE, LANE), LANE)


def rows_of(block, size):
    return pl.ds(pl.multiple_of(block * size, size), size)


def call(kernel, outs, *args, scalars=0, scratch=(), hbm=0, ties=0, limit=16):
    vmem = pl.BlockSpec(memory_space=pltpu.VMEM)
    smem = pl.BlockSpec(memory_space=pltpu.SMEM)
    return pl.pallas_call(
        kernel,
        out_shape=list(outs),
        in_specs=[smem] * scalars + [pl.BlockSpec(memory_space=pltpu.HBM)] * hbm
        + [vmem] * (len(args) - scalars - hbm - ties) + [pl.BlockSpec(memory_space=pl.ANY)] * ties,
        out_specs=[vmem] * len(outs),
        scratch_shapes=list(scratch),
        name=(kernel.func if hasattr(kernel, "func") else kernel).__name__,
        compiler_params=pltpu.CompilerParams(vmem_limit_bytes=limit << 20),
        cost_estimate=pl.CostEstimate(flops=1, bytes_accessed=1, transcendentals=0),
    )(*args)


def after(value, *others):
    return lax.optimization_barrier((value, *others))[0]


def shape(dims, dtype):
    return jax.ShapeDtypeStruct(tuple(dims), dtype)


def adamw(weight, first, second, grad, rate, decay):
    first_new = BETA_FIRST * first + (1.0 - BETA_FIRST) * grad
    second_new = BETA_SECOND * second + (1.0 - BETA_SECOND) * grad * grad
    first_hat = first_new / (1.0 - BETA_FIRST**STEP)
    second_hat = second_new / (1.0 - BETA_SECOND**STEP)
    weight_new = weight - rate * (
        first_hat / (jnp.sqrt(second_hat) + ADAM_EPSILON) + decay * weight
    )
    return (weight_new, first_new, second_new)


def gain_of(gains_ref, which):
    at = 2 * D + which * HD
    return gains_ref[:, at:at + HD]


def tables_kernel(pos_ref, seg_ref, cos_ref, sin_ref, mask_ref):
    length, half = pos_ref.shape[1], HD // 2
    column = jnp.broadcast_to(pos_ref[...].astype(F32), (HD, length)).T
    lane = lax.broadcasted_iota(jnp.int32, (1, HD), 1)
    step = (lane & (half - 1)).astype(F32) * (2.0 / HD)
    angle = column * jnp.exp(step * -math.log(THETA_BASE))
    cos_ref[...] = jnp.cos(angle)
    sine = jnp.sin(angle)
    sin_ref[...] = jnp.where(lane < half, -sine, sine)
    seg = jnp.broadcast_to(seg_ref[...].astype(F32), (length, length))
    i = lax.broadcasted_iota(jnp.int32, (length, length), 0)
    j = lax.broadcasted_iota(jnp.int32, (length, length), 1)
    mask_ref[...] = jnp.where((seg == seg.T) & (j <= i), 1.0, 0.0)


def attend_kernel(n, place, *rest):
    blocks = len(rest) - n - 14
    xs, ws, (gains_ref, cos_ref, sin_ref, mask_ref, ctx_ref, prob_ref, q_ref, k_ref, v_ref, raw_ref, norm_ref, x_ref,
             cot_ref, w_ref) = rest[:n], rest[n:n + blocks], rest[n + blocks:]
    height = D // blocks
    for i, w in enumerate(ws):
        w_ref[i * height:(i + 1) * height, :] = w[...]
    z = place[0]
    part = D // n
    for k in range(n):
        x_ref[:, k * part:(k + 1) * part] = xs[k][:x_ref.shape[0], :]
        cot_ref[:, k * part:(k + 1) * part] = xs[k][x_ref.shape[0]:2 * x_ref.shape[0], :]
    x = x_ref[...].astype(F32)
    r1 = lax.rsqrt(jnp.mean(x * x, axis=-1, keepdims=True) + EPSILON)
    for j in range(BLOCKS):
        b = place[1 + j]
        block = x_ref[:, lanes(b ^ (2 * z))].astype(F32)
        norm_ref[:, j * LANE:(j + 1) * LANE] = (block * r1 * gains_ref[:, lanes(b)]).astype(BF16)
    qw, kw = q_ref.shape[1], k_ref.shape[1]
    qkv = mm(norm_ref[...], w_ref[:, :qw + 2 * kw])
    raw_ref[...] = qkv[:, :qw + kw]
    v_ref[...] = qkv[:, qw + kw:].astype(BF16)
    cosine, sine = cos_ref[...], sin_ref[...]
    for h in range((qw + kw) // HD):
        part = qkv[:, h * HD:(h + 1) * HD]
        is_q = h * HD < qw
        gain = gain_of(gains_ref, 0 if is_q else 1)
        part = part * lax.rsqrt(jnp.mean(part * part, axis=-1, keepdims=True) + EPSILON) * gain
        part = (part * cosine + pltpu.roll(part, HD // 2, 1) * sine).astype(BF16)
        if is_q:
            q_ref[:, h * HD:(h + 1) * HD] = part
        else:
            at = h * HD - qw
            k_ref[:, at:at + HD] = part
    length = x.shape[0]
    allowed = mask_ref[...] > 0.5
    heads, groups = qw // HD, kw // HD
    for h in range(heads):
        g = h * groups // heads
        s = mm_nt(q_ref[:, h * HD:(h + 1) * HD], k_ref[:, g * HD:(g + 1) * HD]) * HD ** (-0.5)
        s = jnp.where(allowed, s, MASK_VALUE)
        peak = jnp.max(s, axis=-1, keepdims=True)
        total = peak + jnp.log(jnp.sum(jnp.exp(s - peak), axis=-1, keepdims=True))
        p = jnp.exp(s - total)
        prob_ref[h * length:(h + 1) * length, :] = p
        ctx_ref[:, h * HD:(h + 1) * HD] = mm(p.astype(BF16), v_ref[:, g * HD:(g + 1) * HD]).astype(BF16)


def branch_kernel(place, ctx_ref, w_ref, own_ref, *rest):
    sends, scratch = rest[:-1], rest[-1]
    z = place[0]
    here = w_ref.shape[1] - ctx_ref.shape[1]
    scratch[...] = mm_nt(ctx_ref[...], w_ref[:, here:])
    size = own_ref.shape[0]
    for k, out in enumerate((own_ref,) + sends):
        to = z ^ k
        for j in range(BLOCKS):
            b = place[1 + j]
            out[:, lanes(b ^ (2 * to))] = scratch[rows_of(to, size), j * LANE:(j + 1) * LANE].astype(out.dtype)


def mid_kernel(n, place, x_ref, gains_ref, *rest):
    terms, (resid_ref, mid_ref) = rest[:n], rest[n:]
    z = place[0]
    size = resid_ref.shape[0]
    resid = x_ref[rows_of(z, size), :].astype(F32)
    total = terms[0][...].astype(F32)
    for term in terms[1:]:
        total = total + term[...].astype(F32)
    resid = resid + total
    resid_ref[...] = resid
    scale = lax.rsqrt(jnp.mean(resid * resid, axis=-1, keepdims=True) + EPSILON)
    for j in range(BLOCKS):
        at = slice(j * LANE, (j + 1) * LANE)
        mid_ref[:, at] = (resid[:, at] * scale * gains_ref[:, lanes(BLOCKS + (j ^ (2 * z)))]).astype(BF16)


def units_math(gate, up, dhidden):
    sigmoid = jax.nn.sigmoid(gate)
    hidden = (gate * sigmoid * up).astype(BF16)
    dgate = (dhidden * up * sigmoid * (1.0 + gate * (1.0 - sigmoid))).astype(BF16)
    dup = (dhidden * gate * sigmoid).astype(BF16)
    return hidden, dgate, dup


def units_kernel(n, place, cot_ref, wz_ref, wo_ref, *rest):
    pieces, outs = rest[:n], rest[n:2 * n]
    mid_ref, hid_ref, dgu_ref, dmid_ref = rest[2 * n:]
    z = place[0]
    size = pieces[0].shape[0]
    part = D // n
    for k in range(n):
        for q in range(n):
            mid_ref[rows_of(z ^ k, size), q * part:(q + 1) * part] = (
                pieces[k][:, (q ^ k) * part:((q ^ k) + 1) * part])
    mid = mid_ref[...]
    cot = cot_ref[...]
    units = wz_ref.shape[1]
    for i, w in enumerate((wz_ref, wo_ref)):
        hidden, dgate, dup = units_math(mm_nt(mid, w[0]), mm_nt(mid, w[1]), mm_nt(cot, w[2]))
        at = slice(i * units, (i + 1) * units)
        hid_ref[:, at] = hidden
        dgu_ref[0, :, at] = dgate
        dgu_ref[1, :, at] = dup
        term = mm(dgate, w[0]) + mm(dup, w[1])
        dmid_ref[...] = term if i == 0 else dmid_ref[...] + term
    for k, out in enumerate(outs):
        out[...] = dmid_ref[rows_of(z ^ k, size), :].astype(out.dtype)


def units_grad_kernel(cot_ref, mid_ref, hid_ref, dgu_ref, gz_ref, go_ref):
    units = gz_ref.shape[1]
    for i, g in ((1, go_ref), (0, gz_ref)):
        at = slice(i * units, (i + 1) * units)
        g[0] = mm_tn(dgu_ref[0, :, at], mid_ref[...]).astype(g.dtype)
        g[1] = mm_tn(dgu_ref[1, :, at], mid_ref[...]).astype(g.dtype)
        g[2] = mm_tn(hid_ref[:, at], cot_ref[...]).astype(g.dtype)


def down_kernel(n, place, hid_ref, wz_ref, wo_ref, resid_ref, *rest):
    outs, total_ref = rest[:n], rest[n]
    units = wz_ref.shape[1]
    size = resid_ref.shape[0]
    total_ref[...] = mm(hid_ref[:, :units], wz_ref[2]) + mm(hid_ref[:, units:], wo_ref[2])
    own = rows_of(place[0], size)
    total_ref[own, :] = total_ref[own, :] + resid_ref[...]
    width = outs[0].shape[1]
    for k, out in enumerate(outs):
        out[...] = total_ref[:, k * width:(k + 1) * width].astype(out.dtype)


def pack_units_kernel(n, place, *rest):
    sources, (x_ref, cot_in_ref), outs, (g, u, d, scratch, sems) = rest[:3], rest[3:5], rest[6:6 + n], rest[6 + n:]
    copies = [pltpu.make_async_copy(src, dst, sems.at[i]) for i, (src, dst) in enumerate(zip(sources, (g, u, d)))]
    for copy in copies:
        copy.start()
    length = 2 * x_ref.shape[0]
    size = (outs[0].shape[0] - length) // 3
    for out in outs:
        out[:length // 2, :] = x_ref[...]
        out[length // 2:length, :] = cot_in_ref[...]
    for i, (copy, ref) in enumerate(zip(copies, (g, u, d))):
        copy.wait()
        scratch[...] = ref[...].T.astype(BF16)
        for k, out in enumerate(outs):
            out[length + i * size:length + (i + 1) * size, :] = scratch[rows_of(place[0] ^ k, size), :]


def join_kernel(n, *rest):
    pieces, out_ref = rest[:n], rest[-1]
    size, width = out_ref.shape[1], pieces[0].shape[1]
    length = pieces[0].shape[0] - 3 * size
    for k, piece in enumerate(pieces):
        for i in range(3):
            out_ref[i, :, k * width:(k + 1) * width] = piece[length + i * size:length + (i + 1) * size, :]


def units_update_kernel(n, place, *rest):
    pieces, states, outs, scratch = rest[:n], rest[n:n + 9], rest[n + 9:n + 18], rest[n + 18]
    size = scratch.shape[0] // n
    length = pieces[0].shape[0] - 3 * size
    for i in range(3):
        for k in range(n):
            scratch[rows_of(place[0] ^ k, size), :] = pieces[k][length + i * size:length + (i + 1) * size, :].astype(F32)
        w, m, v = (ref[...] for ref in states[3 * i:3 * i + 3])
        for ref, value in zip(outs[3 * i:3 * i + 3], adamw(w, m, v, scratch[...].T, MATRIX_RATE, MATRIX_DECAY)):
            ref[...] = value


def update_kernel(n, count, *rest):
    terms, states, outs = rest[:n], rest[n:n + 3 * count], rest[n + 3 * count:]
    total = terms[0][...].astype(F32)
    for term in terms[1:]:
        total = total + term[...].astype(F32)
    at = 0
    for i in range(count):
        w, m, v = (ref[...] for ref in states[3 * i:3 * i + 3])
        grad = total[:, at:at + w.shape[1]]
        at += w.shape[1]
        for ref, value in zip(outs[3 * i:3 * i + 3], adamw(w, m, v, grad, MATRIX_RATE, MATRIX_DECAY)):
            ref[...] = value


def pack_kernel(*rest):
    sources, out_ref, (q, k, v, o, sems) = rest[:4], rest[4], rest[5:]
    copies = [pltpu.make_async_copy(src, dst, sems.at[i]) for i, (src, dst) in enumerate(zip(sources, (q, k, v, o)))]
    for copy in copies:
        copy.start()
    at = 0
    for copy, ref in zip(copies, (q, k, v, o)):
        copy.wait()
        out_ref[:, at:at + ref.shape[1]] = ref[...].astype(BF16)
        at += ref.shape[1]


def mid_back_kernel(n, place, resid_ref, cot_ref, gains_ref, *rest):
    terms, (grad_ref, gain_ref, dmid_ref) = rest[:n], rest[n:]
    z = place[0]
    part = D // n
    for k, term in enumerate(terms):
        for q in range(n):
            at = slice(q * part, (q + 1) * part)
            value = term[:, (q ^ k) * part:((q ^ k) + 1) * part].astype(F32)
            dmid_ref[:, at] = value if k == 0 else dmid_ref[:, at] + value
    dmid = dmid_ref[...]
    resid = resid_ref[...]
    cot = cot_ref[rows_of(z, resid.shape[0]), :].astype(F32)
    r2 = lax.rsqrt(jnp.mean(resid * resid, axis=-1, keepdims=True) + EPSILON)
    inner = None
    for j in range(BLOCKS):
        at = slice(j * LANE, (j + 1) * LANE)
        b = j ^ (2 * z)
        part = dmid[:, at] * gains_ref[:, lanes(BLOCKS + b)] * resid[:, at]
        inner = part if inner is None else inner + part
        gain_ref[:, lanes(b)] = jnp.sum(dmid[:, at] * resid[:, at] * r2, axis=0, keepdims=True)
    inner = jnp.sum(inner, axis=-1, keepdims=True)
    back = r2 * r2 * r2 * inner / D
    for j in range(BLOCKS):
        at = slice(j * LANE, (j + 1) * LANE)
        grad_ref[:, at] = (
            cot[:, at] + r2 * gains_ref[:, lanes(BLOCKS + (j ^ (2 * z)))] * dmid[:, at] - resid[:, at] * back
        ).astype(BF16)


def attend_back_kernel(n, place, *rest):
    pieces, (w_ref, prob_ref, q_ref, k_ref, v_ref, raw_ref, gains_ref, cos_ref, sin_ref,
             dqkv_ref, dgq_ref, dgk_ref, dbr_ref) = rest[:n], rest[n:]
    z = place[0]
    size = pieces[0].shape[0]
    for k in range(n):
        frm = z ^ k
        for j in range(BLOCKS):
            b = place[1 + j]
            dbr_ref[rows_of(frm, size), j * LANE:(j + 1) * LANE] = pieces[k][:, lanes(b ^ (2 * frm))]
    here = dqkv_ref.shape[1]
    dctx = mm(dbr_ref[...], w_ref[:, here:]).astype(BF16)
    qw, kw = q_ref.shape[1], k_ref.shape[1]
    heads, groups = qw // HD, kw // HD
    length = dbr_ref.shape[0]
    cosine, sine = cos_ref[...], sin_ref[...]

    def back(grad, h, gain):
        grad = grad * cosine - pltpu.roll(grad, HD // 2, 1) * sine
        value = raw_ref[:, h * HD:(h + 1) * HD]
        factor = lax.rsqrt(jnp.mean(value * value, axis=-1, keepdims=True) + EPSILON)
        inner = jnp.sum(grad * gain * value, axis=-1, keepdims=True)
        out = factor * gain * grad - value * (factor * factor * factor) * inner / HD
        return out.astype(BF16), jnp.sum(grad * value * factor, axis=0, keepdims=True)

    dgq = dgk = None
    for g in range(groups):
        dk = dv = None
        keys = k_ref[:, g * HD:(g + 1) * HD]
        vals = v_ref[:, g * HD:(g + 1) * HD]
        for h in range(g * heads // groups, (g + 1) * heads // groups):
            hs = slice(h * HD, (h + 1) * HD)
            p = prob_ref[h * length:(h + 1) * length, :]
            dp = mm_nt(dctx[:, hs], vals)
            delta = jnp.sum(p * dp, axis=-1, keepdims=True)
            ds = (p * (dp - delta)).astype(BF16)
            dq, gain_part = back(mm(ds, keys) * HD ** (-0.5), h, gain_of(gains_ref, 0))
            dqkv_ref[:, hs] = dq
            dgq = gain_part if dgq is None else dgq + gain_part
            dk_h = mm_tn(ds, q_ref[:, hs])
            dv_h = mm_tn(p.astype(BF16), dctx[:, hs])
            dk = dk_h if dk is None else dk + dk_h
            dv = dv_h if dv is None else dv + dv_h
        dk, gain_part = back(dk * HD ** (-0.5), heads + g, gain_of(gains_ref, 1))
        dgk = gain_part if dgk is None else dgk + gain_part
        dqkv_ref[:, qw + g * HD:qw + (g + 1) * HD] = dk
        dqkv_ref[:, qw + kw + g * HD:qw + kw + (g + 1) * HD] = dv.astype(BF16)
    dgq_ref[...] = dgq
    dgk_ref[...] = dgk


def weight_grad_kernel(norm_ref, dqkv_ref, dbr_ref, ctx_ref, gz_ref, *outs):
    half = D // 2
    here = dqkv_ref.shape[1]
    step = half // len(outs)
    for left, right, cols in ((norm_ref, dqkv_ref, slice(0, here)), (dbr_ref, ctx_ref, slice(here, None))):
        other = mm_tn(left[:, half:], right[...]).astype(BF16)
        for i, out in enumerate(outs):
            out[:, cols] = other[i * step:(i + 1) * step, :]
    gz_ref[:, :here] = mm_tn(norm_ref[:, :half], dqkv_ref[...])
    gz_ref[:, here:] = mm_tn(dbr_ref[:, :half], ctx_ref[...])


def pair_sum_kernel(n, own_ref, *rest):
    others, outs = rest[:n], rest[n:]
    step = own_ref.shape[0] // n
    for i, (other, out) in enumerate(zip(others, outs)):
        out[...] = (own_ref[i * step:(i + 1) * step, :] + other[...].astype(F32)).astype(out.dtype)


def input_grad_kernel(n, count, place, dqkv_ref, w_ref, x_ref, gains_ref, *rest):
    units, rest = rest[:count], rest[count + 1:]
    outs, gain_ref, dn_ref, term_ref = rest[:n], rest[n], rest[n + 1], rest[n + 2]
    z = place[0]
    dn_ref[...] = mm_nt(dqkv_ref[...], w_ref[:, :dqkv_ref.shape[1]])
    x = x_ref[...].astype(F32)
    r1 = lax.rsqrt(jnp.mean(x * x, axis=-1, keepdims=True) + EPSILON)
    inner = None
    for j in range(BLOCKS):
        b = place[1 + j]
        dn = dn_ref[:, j * LANE:(j + 1) * LANE]
        xb = x_ref[:, lanes(b ^ (2 * z))].astype(F32)
        part = dn * gains_ref[:, lanes(b)] * xb
        inner = part if inner is None else inner + part
        gain_ref[:, lanes(b)] = jnp.sum(dn * xb * r1, axis=0, keepdims=True)
    inner = jnp.sum(inner, axis=-1, keepdims=True)
    back = r1 * r1 * r1 * inner / D
    for j in range(BLOCKS):
        b = place[1 + j]
        at = lanes(b ^ (2 * z))
        xb = x_ref[:, at].astype(F32)
        term_ref[:, at] = r1 * gains_ref[:, lanes(b)] * dn_ref[:, j * LANE:(j + 1) * LANE] - xb * back
    width = outs[0].shape[1]
    length = x.shape[0]
    for k, out in enumerate(outs):
        out[:length, :] = term_ref[:, k * width:(k + 1) * width].astype(out.dtype)
    if count:
        size = units[0].shape[1]
        for i in range(3):
            total = units[0][i]
            for unit in units[1:]:
                total = total + unit[i].astype(F32)
            for k, out in enumerate(outs):
                out[length + i * size:length + (i + 1) * size, :] = total[:, k * width:(k + 1) * width].astype(out.dtype)


def act_grad_kernel(n, place, *rest):
    pieces, terms, out_ref = rest[:n], rest[n:2 * n], rest[2 * n]
    z = place[0]
    width = out_ref.shape[1]
    size = pieces[0].shape[0]
    for k in range(n):
        at = rows_of(z ^ k, size)
        total = terms[0][at, :].astype(F32)
        for term in terms[1:]:
            total = total + term[at, :].astype(F32)
        out_ref[at, :] = pieces[k][:, k * width:(k + 1) * width].astype(F32) + total


def act_out_kernel(*rest):
    terms, out_ref = rest[:-1], rest[-1]
    total = terms[0][...].astype(F32)
    for term in terms[1:]:
        total = total + term[...].astype(F32)
    out_ref[...] = total.astype(BF16)


def body(sizes, act_in, act_cot, segments, positions, gains, gains_first, gains_second,
         query_weight, query_first, query_second, key_weight, key_first, key_second,
         value_weight, value_first, value_second, output_weight, output_first, output_second,
         gate_weight, gate_first, gate_second, up_weight, up_first, up_second,
         down_weight, down_first, down_second):
    n_dp, n_row, n_col = sizes
    n_plane = n_dp * n_col
    paired = n_dp == 2 and n_col == 4
    z = lax.axis_index("row").astype(jnp.int32)
    p = lax.axis_index(PLANE).astype(jnp.int32)

    def over_row(value, k):
        return lax.ppermute(value, "row", [(i, i ^ k) for i in range(n_row)])

    def over_plane(value, k):
        return lax.ppermute(value, PLANE, [(i, i ^ k) for i in range(n_plane)])

    def gather_row(value):
        return [value] + [over_row(value, k) for k in range(1, n_row)]

    def scatter_row(values):
        return [values[0]] + [over_row(values[k], k) for k in range(1, n_row)]

    def near_plane(value, axis=0):
        if not paired:
            return lax.all_gather(value, PLANE, axis=axis, tiled=True)
        return jnp.concatenate([value] + [over_plane(value, k) for k in (2, 4, 6)], axis=axis)

    def far_plane(same, axis=0):
        if not paired:
            return tuple(jnp.split(same, 2, axis=axis))
        return same, over_plane(same, 1)

    def gather_plane(value, axis=0):
        return far_plane(near_plane(value, axis), axis)

    def pair_plane(same, other, axis=0):
        if not paired:
            whole = jnp.concatenate([same.astype(F32), other.astype(F32)], axis=axis)
            return [lax.psum_scatter(whole, PLANE, scatter_dimension=axis, tiled=True)]
        total = same.astype(F32) + over_plane(other, 1).astype(F32)
        parts = jnp.split(total, 4, axis=axis)
        return parts[:1] + [part.astype(BF16) for part in parts[1:]]

    def rest_plane(parts):
        return list(parts[:1]) + [over_plane(part, k) for part, k in zip(parts[1:], (2, 4, 6))]

    def add(terms):
        out = terms[0].astype(F32)
        for term in terms[1:]:
            out = out + term.astype(F32)
        return out

    def sum_all(value):
        if not paired:
            return lax.psum(value, ("dp", "row", "col"))
        value = value + over_plane(value, 1)
        value = value + over_plane(value, 2) + over_plane(value, 4) + over_plane(value, 6)
        return value + over_row(value, 1) + over_row(value, 2) + over_row(value, 3)

    order = jnp.array([0, 2, 4, 6, 1, 3, 5, 7], jnp.int32) ^ p if paired else jnp.arange(BLOCKS, dtype=jnp.int32)
    place = jnp.concatenate([z[None], order])

    length, width = act_in.shape
    size = length // n_row
    qw, kw = query_weight.shape[1], key_weight.shape[1]
    rows = query_weight.shape[0]
    units = gate_weight.shape[1]
    gain = gains[None, :]
    if rows % 16 == 0:
        (w_proj,) = call(
            pack_kernel, [shape((rows, 2 * qw + 2 * kw), BF16)],
            query_weight, key_weight, value_weight, output_weight, hbm=4, limit=56,
            scratch=[pltpu.VMEM((rows, w), F32) for w in (qw, kw, kw, qw)] + [pltpu.SemaphoreType.DMA((4,))])
    else:
        w_proj = jnp.concatenate([query_weight, key_weight, value_weight, output_weight], axis=1).astype(BF16)
    if paired:
        near = [w_proj] + [over_plane(w_proj, k) for k in (2, 4, 6)]
    else:
        near = list(jnp.split(lax.all_gather(w_proj, PLANE, axis=0, tiled=True), 2, axis=0))
    share = units // n_row
    small = share % 16 != 0
    if small:
        joined = jnp.stack([gate_weight, up_weight, down_weight]).astype(BF16).transpose(0, 2, 1)
        parts = [lax.dynamic_slice_in_dim(joined, (z ^ k) * share, share, 1) for k in range(n_row)]
        units_mine = jnp.concatenate(scatter_row(parts), axis=2)
        xs = gather_row(jnp.concatenate([act_in, act_cot], axis=0))
    else:
        xs = call(
            functools.partial(pack_units_kernel, n_row), [shape((2 * length + 3 * share, width), BF16)] * n_row,
            place, gate_weight, up_weight, down_weight, act_in, act_cot, w_proj, scalars=1, hbm=3, ties=1, limit=48,
            scratch=[pltpu.VMEM((width, units), F32)] * 3
            + [pltpu.VMEM((units, width), BF16), pltpu.SemaphoreType.DMA((3,))])
        xs = scatter_row(xs)
    cosine, sine, mask = call(
        tables_kernel, [shape((length, HD), F32)] * 2 + [shape((length, length), F32)],
        positions[None, :], segments[None, :])
    w_parts = near + [over_plane(part, 1) for part in near] if paired else near

    heads = qw // HD
    context, probs, queries, keys, values, raw, normed, x_row, cot_row, w_proj = call(
        functools.partial(attend_kernel, n_row),
        [shape((length, qw), BF16), shape((heads * length, length), F32), shape((length, qw), BF16),
         shape((length, kw), BF16), shape((length, kw), BF16), shape((length, qw + kw), F32),
         shape((length, D), BF16), shape((length, D), BF16), shape((length, D), BF16),
         shape((D, 2 * qw + 2 * kw), BF16)],
        place, *xs, *w_parts, gain, cosine, sine, mask, scalars=1)
    if not small:
        (units_mine,) = call(functools.partial(join_kernel, n_row), [shape((3, share, D), BF16)],
                             *xs)
    units_near = near_plane(units_mine, axis=1)
    terms = call(
        branch_kernel,
        [shape((size, D), F32)] + [shape((size, D), BF16)] * (n_row - 1),
        place, context, w_proj,
        scalars=1, scratch=[pltpu.VMEM((length, D), F32)])
    terms = scatter_row(terms)
    resid, mid = call(
        functools.partial(mid_kernel, n_row),
        [shape((size, D), F32), shape((size, D), BF16)],
        place, x_row, gain, *terms, scalars=1)

    mids = gather_row(mid)
    units_z, units_o = far_plane(after(units_near, mid), axis=1)
    here = 2 * units_z.shape[1]
    *dmid_terms, mid_all, hidden, d_units = call(
        functools.partial(units_kernel, n_row),
        [shape((size, D), F32 if k == 0 else BF16) for k in range(n_row)]
        + [shape((length, D), BF16), shape((length, here), BF16), shape((2, length, here), BF16)],
        place, cot_row, units_z, units_o, *mids,
        scalars=1, scratch=[pltpu.VMEM((length, D), F32)])
    dmid_terms = scatter_row(dmid_terms)
    unit_grad_z, unit_grad_o = call(
        units_grad_kernel, [shape(units_z.shape, BF16)] * 2,
        cot_row, mid_all, hidden, d_units)
    unit_pair = pair_plane(unit_grad_z, unit_grad_o, axis=1)
    resid = after(resid, *unit_pair)
    unit_terms = rest_plane(unit_pair)
    branch_grad, mid_gain_grad = call(
        functools.partial(mid_back_kernel, n_row),
        [shape((size, D), BF16), shape((1, D), F32)],
        place, resid, cot_row, gain, *dmid_terms,
        scalars=1, scratch=[pltpu.VMEM((size, D), F32)])

    pieces = gather_row(branch_grad)
    down_terms = call(
        functools.partial(down_kernel, n_row),
        [shape((length, width), F32 if k == 0 else BF16) for k in range(n_row)],
        place, hidden, units_z, units_o, resid,
        scalars=1, scratch=[pltpu.VMEM((length, D), F32)])
    down_terms = scatter_row([after(term, *pieces) for term in down_terms])
    (act_out,) = call(act_out_kernel, [shape((length, width), BF16)], *down_terms)
    dqkv, query_gain_grad, key_gain_grad, dbranch = call(
        functools.partial(attend_back_kernel, n_row),
        [shape((length, qw + 2 * kw), BF16), shape((1, HD), F32), shape((1, HD), F32), shape((length, D), BF16)],
        place, *pieces, w_proj, probs, queries, keys, values, raw, gain, cosine, sine, scalars=1)
    merged = [] if small else unit_terms
    count = length if small else length + 3 * share
    *in_terms, in_gain_grad = call(
        functools.partial(input_grad_kernel, n_row, len(merged)),
        [shape((count, width), F32 if k == 0 else BF16) for k in range(n_row)] + [shape((1, D), F32)],
        place, dqkv, w_proj, x_row, gain, *merged, act_out,
        scalars=1, scratch=[pltpu.VMEM((length, D), F32)] * 2)
    cols = 2 * qw + 2 * kw
    grad_own, *grad_others = call(
        weight_grad_kernel,
        [shape((D // 2, cols), F32)] + [shape((D // 2 // 4, cols), BF16)] * 4,
        normed, dqkv, dbranch, after(context, in_terms[0]))
    if paired:
        grad_others = [over_plane(part, 1) for part in grad_others]
        proj_pair = call(functools.partial(pair_sum_kernel, 4),
                         [shape((rows, cols), F32 if i == 0 else BF16) for i in range(4)], grad_own, *grad_others)
        proj_terms = rest_plane(proj_pair)
    else:
        proj_pair = proj_terms = pair_plane(grad_own, jnp.concatenate(grad_others, axis=0))
    in_terms = scatter_row(in_terms)
    gains_grad = jnp.concatenate([in_gain_grad, mid_gain_grad, query_gain_grad, key_gain_grad], axis=1)
    gains_grad = sum_all(after(gains_grad, *proj_pair))[0]

    (act_grad,) = call(functools.partial(act_grad_kernel, n_row), [shape((length, width), F32)],
                       place, *pieces, *in_terms, scalars=1)
    states = (gate_weight, gate_first, gate_second, up_weight, up_first, up_second,
              down_weight, down_first, down_second)
    if small:
        unit_parts = scatter_row(jnp.split(add(unit_terms).astype(BF16), n_row, axis=2))
        whole = jnp.zeros((3, units, width), F32)
        for k, part in enumerate(unit_parts):
            whole = lax.dynamic_update_slice_in_dim(whole, part.astype(F32), (z ^ k) * share, 1)
        new_units = []
        for i in range(3):
            new_units += adamw(*states[3 * i:3 * i + 3], whole[i].T, MATRIX_RATE, MATRIX_DECAY)
    else:
        new_units = call(functools.partial(units_update_kernel, n_row), [shape((width, units), F32)] * 9,
                         place, *in_terms, *states,
                         scalars=1, scratch=[pltpu.VMEM((units, width), F32)])

    def update(terms, *states):
        return call(functools.partial(update_kernel, len(terms), len(states) // 3),
                    [shape(state.shape, F32) for state in states], *terms, *states)

    return (
        act_out,
        act_grad,
        *adamw(gains, gains_first, gains_second, gains_grad, GAIN_RATE, 0.0),
        *update(proj_terms, query_weight, query_first, query_second, key_weight, key_first, key_second,
                value_weight, value_first, value_second, output_weight, output_first, output_second),
        *new_units,
    )


def solution(mesh):
    token, proj, unit = P(PLANE, "row"), P(PLANE, "row"), P("row", PLANE)
    sizes = (mesh.shape["dp"], mesh.shape["row"], mesh.shape["col"])
    return jax.shard_map(
        functools.partial(body, sizes),
        mesh=mesh,
        in_specs=(token, token, P(PLANE), P(PLANE)) + (P(),) * 3 + (proj,) * 12 + (unit,) * 9,
        out_specs=(token, token) + (P(),) * 3 + (proj,) * 12 + (unit,) * 9,
        check_vma=False,
    )
```

```python
import functools
import math

import jax
import jax.numpy as jnp
from jax import lax
from jax.experimental import pallas as pl
from jax.experimental.pallas import tpu as pltpu
from jax.sharding import PartitionSpec as P

D = 1024
HD = 128
STEP = 10

EPSILON = 1e-06
THETA_BASE = 1000000.0
BETA_FIRST = 0.9
BETA_SECOND = 0.95
ADAM_EPSILON = 1e-08
MATRIX_RATE = 0.04
MATRIX_DECAY = 0.1
GAIN_RATE = 0.5
MASK_VALUE = -1e30
LANE = 128
BLOCKS = D // LANE
ATTEND_LIMIT = 40
UPDATE_LIMIT = 16
GAIN_ROWS = 16
PLANE = ("dp", "col")
F32 = jnp.float32
BF16 = jnp.bfloat16


def mm(left, right):
    return jnp.dot(left, right, preferred_element_type=F32)


def mm_nt(left, right):
    return lax.dot_general(left, right, (((1,), (1,)), ((), ())), preferred_element_type=F32)


def mm_tn(left, right):
    return lax.dot_general(left, right, (((0,), (0,)), ((), ())), preferred_element_type=F32)


def lanes(block):
    return pl.ds(pl.multiple_of(block * LANE, LANE), LANE)


def rows_of(block, size):
    return pl.ds(pl.multiple_of(block * size, size), size)


def call(kernel, outs, *args, scalars=0, scratch=(), hbm=0, ties=0, limit=16):
    vmem = pl.BlockSpec(memory_space=pltpu.VMEM)
    smem = pl.BlockSpec(memory_space=pltpu.SMEM)
    return pl.pallas_call(
        kernel,
        out_shape=list(outs),
        in_specs=[smem] * scalars + [pl.BlockSpec(memory_space=pltpu.HBM)] * hbm
        + [vmem] * (len(args) - scalars - hbm - ties) + [pl.BlockSpec(memory_space=pl.ANY)] * ties,
        out_specs=[vmem] * len(outs),
        scratch_shapes=list(scratch),
        name=(kernel.func if hasattr(kernel, "func") else kernel).__name__,
        compiler_params=pltpu.CompilerParams(vmem_limit_bytes=limit << 20),
        cost_estimate=pl.CostEstimate(flops=1, bytes_accessed=1, transcendentals=0),
    )(*args)


def after(value, *others):
    return lax.optimization_barrier((value, *others))[0]


def shape(dims, dtype):
    return jax.ShapeDtypeStruct(tuple(dims), dtype)


def adamw(weight, first, second, grad, rate, decay):
    first_new = BETA_FIRST * first + (1.0 - BETA_FIRST) * grad
    second_new = BETA_SECOND * second + (1.0 - BETA_SECOND) * grad * grad
    first_hat = first_new * (1.0 / (1.0 - BETA_FIRST**STEP))
    second_hat = second_new * (1.0 / (1.0 - BETA_SECOND**STEP))
    weight_new = weight - rate * (
        first_hat / (jnp.sqrt(second_hat) + ADAM_EPSILON) + decay * weight
    )
    return (weight_new, first_new, second_new)


def gain_of(gains_ref, which):
    at = 2 * D + which * HD
    return gains_ref[:, at:at + HD]


def tables_kernel(pos_ref, seg_ref, cos_ref, sin_ref, mask_ref):
    length, half = pos_ref.shape[1], HD // 2
    column = jnp.broadcast_to(pos_ref[...].astype(F32), (HD, length)).T
    lane = lax.broadcasted_iota(jnp.int32, (1, HD), 1)
    step = (lane & (half - 1)).astype(F32) * (2.0 / HD)
    angle = column * jnp.exp(step * -math.log(THETA_BASE))
    cos_ref[...] = jnp.cos(angle)
    sine = jnp.sin(angle)
    sin_ref[...] = jnp.where(lane < half, -sine, sine)
    seg = jnp.broadcast_to(seg_ref[...].astype(F32), (length, length))
    i = lax.broadcasted_iota(jnp.int32, (length, length), 0)
    j = lax.broadcasted_iota(jnp.int32, (length, length), 1)
    mask_ref[...] = jnp.where((seg == seg.T) & (j <= i), 1.0, 0.0)


def attend_kernel(n, place, *rest):
    blocks = len(rest) - n - 14
    xs, ws, (gains_ref, cos_ref, sin_ref, mask_ref, ctx_ref, prob_ref, q_ref, k_ref, v_ref, raw_ref, norm_ref, x_ref,
             cot_ref, w_ref) = rest[:n], rest[n:n + blocks], rest[n + blocks:]
    height = D // blocks
    for i, w in enumerate(ws):
        w_ref[i * height:(i + 1) * height, :] = w[0]
    z = place[0]
    part = D // n
    for k in range(n):
        x_ref[:, k * part:(k + 1) * part] = xs[k][:x_ref.shape[0], :]
        cot_ref[:, k * part:(k + 1) * part] = xs[k][x_ref.shape[0]:2 * x_ref.shape[0], :]
    x = x_ref[...].astype(F32)
    r1 = lax.rsqrt(jnp.mean(x * x, axis=-1, keepdims=True) + EPSILON)
    for j in range(BLOCKS):
        b = place[1 + j]
        block = x_ref[:, lanes(b ^ (2 * z))].astype(F32)
        norm_ref[:, j * LANE:(j + 1) * LANE] = (block * r1 * gains_ref[:, lanes(b)]).astype(BF16)
    qw, kw = q_ref.shape[1], k_ref.shape[1]
    qkv = mm(norm_ref[...], w_ref[:, :qw + 2 * kw])
    raw_ref[...] = qkv[:, :qw + kw]
    v_ref[...] = qkv[:, qw + kw:].astype(BF16)
    cosine, sine = cos_ref[...], sin_ref[...]
    for h in range((qw + kw) // HD):
        part = qkv[:, h * HD:(h + 1) * HD]
        is_q = h * HD < qw
        gain = gain_of(gains_ref, 0 if is_q else 1)
        part = part * lax.rsqrt(jnp.mean(part * part, axis=-1, keepdims=True) + EPSILON) * gain
        part = (part * cosine + pltpu.roll(part, HD // 2, 1) * sine).astype(BF16)
        if is_q:
            q_ref[:, h * HD:(h + 1) * HD] = part
        else:
            at = h * HD - qw
            k_ref[:, at:at + HD] = part
    length = x.shape[0]
    allowed = mask_ref[...] > 0.5
    heads, groups = qw // HD, kw // HD
    for h in range(heads):
        g = h * groups // heads
        s = mm_nt(q_ref[:, h * HD:(h + 1) * HD], k_ref[:, g * HD:(g + 1) * HD]) * HD ** (-0.5)
        s = jnp.where(allowed, s, MASK_VALUE)
        peak = jnp.max(s, axis=-1, keepdims=True)
        total = peak + jnp.log(jnp.sum(jnp.exp(s - peak), axis=-1, keepdims=True))
        p = jnp.exp(s - total)
        prob_ref[h * length:(h + 1) * length, :] = p
        ctx_ref[:, h * HD:(h + 1) * HD] = mm(p.astype(BF16), v_ref[:, g * HD:(g + 1) * HD]).astype(BF16)


def branch_kernel(place, ctx_ref, w_ref, own_ref, *rest):
    sends, scratch = rest[:-1], rest[-1]
    z = place[0]
    here = w_ref.shape[1] - ctx_ref.shape[1]
    scratch[...] = mm_nt(ctx_ref[...], w_ref[:, here:])
    size = own_ref.shape[0]
    for k, out in enumerate((own_ref,) + sends):
        to = z ^ k
        for j in range(BLOCKS):
            b = place[1 + j]
            out[:, lanes(b ^ (2 * to))] = scratch[rows_of(to, size), j * LANE:(j + 1) * LANE].astype(out.dtype)


def mid_kernel(n, place, x_ref, gains_ref, *rest):
    terms, (resid_ref, mid_ref) = rest[:n], rest[n:]
    z = place[0]
    size = resid_ref.shape[0]
    resid = x_ref[rows_of(z, size), :].astype(F32)
    total = terms[0][...].astype(F32)
    for term in terms[1:]:
        total = total + term[...].astype(F32)
    resid = resid + total
    resid_ref[...] = resid
    scale = lax.rsqrt(jnp.mean(resid * resid, axis=-1, keepdims=True) + EPSILON)
    for j in range(BLOCKS):
        at = slice(j * LANE, (j + 1) * LANE)
        mid_ref[:, at] = (resid[:, at] * scale * gains_ref[:, lanes(BLOCKS + (j ^ (2 * z)))]).astype(BF16)


def units_math(gate, up, dhidden):
    sigmoid = jax.nn.sigmoid(gate)
    hidden = (gate * sigmoid * up).astype(BF16)
    dgate = (dhidden * up * sigmoid * (1.0 + gate * (1.0 - sigmoid))).astype(BF16)
    dup = (dhidden * gate * sigmoid).astype(BF16)
    return hidden, dgate, dup


def units_kernel(n, place, cot_ref, wz_ref, wo_ref, *rest):
    pieces, outs = rest[:n], rest[n:2 * n]
    mid_ref, hid_ref, dgu_ref, dmid_ref = rest[2 * n:]
    z = place[0]
    size = pieces[0].shape[0]
    part = D // n
    for k in range(n):
        for q in range(n):
            mid_ref[rows_of(z ^ k, size), q * part:(q + 1) * part] = (
                pieces[k][:, (q ^ k) * part:((q ^ k) + 1) * part])
    mid = mid_ref[...]
    cot = cot_ref[...]
    units = wz_ref.shape[1]
    for i, w in enumerate((wz_ref, wo_ref)):
        hidden, dgate, dup = units_math(mm_nt(mid, w[0]), mm_nt(mid, w[1]), mm_nt(cot, w[2]))
        at = slice(i * units, (i + 1) * units)
        hid_ref[:, at] = hidden
        dgu_ref[0, :, at] = dgate
        dgu_ref[1, :, at] = dup
        term = mm(dgate, w[0]) + mm(dup, w[1])
        dmid_ref[...] = term if i == 0 else dmid_ref[...] + term
    for k, out in enumerate(outs):
        out[...] = dmid_ref[rows_of(z ^ k, size), :].astype(out.dtype)


def units_grad_kernel(cot_ref, mid_ref, hid_ref, dgu_ref, gz_ref, go_ref):
    units = gz_ref.shape[1]
    for i, g in ((1, go_ref), (0, gz_ref)):
        at = slice(i * units, (i + 1) * units)
        g[0] = mm_tn(dgu_ref[0, :, at], mid_ref[...]).astype(g.dtype)
        g[1] = mm_tn(dgu_ref[1, :, at], mid_ref[...]).astype(g.dtype)
        g[2] = mm_tn(hid_ref[:, at], cot_ref[...]).astype(g.dtype)


def down_kernel(n, place, hid_ref, wz_ref, wo_ref, resid_ref, *rest):
    outs, total_ref = rest[:n], rest[n]
    units = wz_ref.shape[1]
    size = resid_ref.shape[0]
    total_ref[...] = mm(hid_ref[:, :units], wz_ref[2]) + mm(hid_ref[:, units:], wo_ref[2])
    own = rows_of(place[0], size)
    total_ref[own, :] = total_ref[own, :] + resid_ref[...]
    width = outs[0].shape[1]
    for k, out in enumerate(outs):
        out[...] = total_ref[:, k * width:(k + 1) * width].astype(out.dtype)


def pack_kernel(n, *rest):
    z = lax.axis_index("row")
    sources, out_ref, outs, buffers = rest[:9], rest[9], rest[10:10 + n], rest[10 + n:]
    (*held, scratch, sems) = buffers
    copies = [pltpu.make_async_copy(src, dst, sems.at[i]) for i, (src, dst) in enumerate(zip(sources, held))]
    for copy in copies:
        copy.start()
    at = 0
    for copy, ref in zip(copies[:4], held[:4]):
        copy.wait()
        out_ref[0, :, at:at + ref.shape[1]] = ref[...].astype(BF16)
        at += ref.shape[1]
    x, cot = held[4:6]
    length = 2 * x.shape[0]
    size = (outs[0].shape[0] - length) // 3
    copies[4].wait()
    copies[5].wait()
    for out in outs:
        out[:length // 2, :] = x[...]
        out[length // 2:length, :] = cot[...]
    for i, (copy, ref) in enumerate(zip(copies[6:], held[6:])):
        copy.wait()
        scratch[...] = ref[...].T.astype(BF16)
        for k, out in enumerate(outs):
            out[length + i * size:length + (i + 1) * size, :] = scratch[rows_of(z ^ k, size), :]


def join_kernel(n, *rest):
    pieces, out_ref = rest[:n], rest[-1]
    size, width = out_ref.shape[1], pieces[0].shape[1]
    length = pieces[0].shape[0] - 3 * size
    for k, piece in enumerate(pieces):
        for i in range(3):
            out_ref[i, :, k * width:(k + 1) * width] = piece[length + i * size:length + (i + 1) * size, :]


def pair_sum_kernel(own_ref, *rest):
    others, (keep_ref, keep_x, keep_y, send_x, send_y) = rest[:-5], rest[-5:]
    lead, size, cols = keep_ref.shape
    half = cols // 2

    def block(i, at):
        rows = slice(i * size, (i + 1) * size)
        other = others[0][:, rows, at] if len(others) == 1 else others[i][:, :, at]
        return own_ref[:, rows, at].astype(F32) + other.astype(F32)

    first, second = slice(0, half), slice(half, cols)
    send_x[:lead] = block(1, first).astype(BF16)
    send_x[lead:] = block(3, first).astype(BF16)
    send_y[:lead] = block(2, second).astype(BF16)
    send_y[lead:] = block(3, second).astype(BF16)
    keep_ref[...] = block(0, slice(0, cols))
    keep_x[...] = block(1, second)
    keep_y[...] = block(2, first)


def block_sum_kernel(own_ref, other_ref, *outs):
    size = outs[0].shape[1]
    for i, out in enumerate(outs):
        rows = slice(i * size, (i + 1) * size)
        out[...] = (own_ref[:, rows, :].astype(F32) + other_ref[:, rows, :].astype(F32)).astype(out.dtype)


def relay_sum_kernel(keep_x, keep_y, got_x, got_y, send_x, send_y):
    lead = keep_x.shape[0]
    send_y[...] = (keep_y[...] + got_x[lead:].astype(F32)).astype(BF16)
    send_x[...] = (keep_x[...] + got_y[lead:].astype(F32)).astype(BF16)


def plane_total(terms, i):
    if len(terms) != 5:
        total = terms[0][i].astype(F32)
        for term in terms[1:]:
            total = total + term[i].astype(F32)
        return total
    keep, got_x, got_y, last_x, last_y = terms
    half = keep.shape[2] // 2
    first = keep[i, :, :half] + (got_x[i].astype(F32) + last_y[i].astype(F32))
    second = keep[i, :, half:] + (got_y[i].astype(F32) + last_x[i].astype(F32))
    return jnp.concatenate([first, second], axis=1)


def units_update_kernel(n, place, *rest):
    pieces, states, outs, scratch = rest[:n], rest[n:n + 9], rest[n + 9:n + 18], rest[n + 18]
    size = scratch.shape[0] // n
    base = pieces[0].shape[0] - 3 * size
    for i in range(3):
        for k in range(n):
            scratch[rows_of(place[0] ^ k, size), :] = pieces[k][base + i * size:base + (i + 1) * size, :].astype(F32)
        w, m, v = (ref[...] for ref in states[3 * i:3 * i + 3])
        for ref, value in zip(outs[3 * i:3 * i + 3], adamw(w, m, v, scratch[...].T, MATRIX_RATE, MATRIX_DECAY)):
            ref[...] = value


def update_kernel(n, count, *rest):
    terms, states, outs = rest[:n], rest[n:n + 3 * count], rest[n + 3 * count:]
    total = plane_total(terms, 0)
    at = 0
    for i in range(count):
        w, m, v = (ref[...] for ref in states[3 * i:3 * i + 3])
        grad = total[:, at:at + w.shape[1]]
        at += w.shape[1]
        for ref, value in zip(outs[3 * i:3 * i + 3], adamw(w, m, v, grad, MATRIX_RATE, MATRIX_DECAY)):
            ref[...] = value


def mid_back_kernel(n, place, resid_ref, cot_ref, gains_ref, *rest):
    terms, (grad_ref, gain_ref, dmid_ref) = rest[:n], rest[n:]
    z = place[0]
    part = D // n
    for k, term in enumerate(terms):
        for q in range(n):
            at = slice(q * part, (q + 1) * part)
            value = term[:, (q ^ k) * part:((q ^ k) + 1) * part].astype(F32)
            dmid_ref[:, at] = value if k == 0 else dmid_ref[:, at] + value
    dmid = dmid_ref[...]
    resid = resid_ref[...]
    cot = cot_ref[rows_of(z, resid.shape[0]), :].astype(F32)
    r2 = lax.rsqrt(jnp.mean(resid * resid, axis=-1, keepdims=True) + EPSILON)
    inner = None
    for j in range(BLOCKS):
        at = slice(j * LANE, (j + 1) * LANE)
        b = j ^ (2 * z)
        part = dmid[:, at] * gains_ref[:, lanes(BLOCKS + b)] * resid[:, at]
        inner = part if inner is None else inner + part
        gain_ref[:, lanes(b)] = jnp.sum(dmid[:, at] * resid[:, at] * r2, axis=0, keepdims=True)
    inner = jnp.sum(inner, axis=-1, keepdims=True)
    back = r2 * r2 * r2 * inner / D
    for j in range(BLOCKS):
        at = slice(j * LANE, (j + 1) * LANE)
        grad_ref[:, at] = (
            cot[:, at] + r2 * gains_ref[:, lanes(BLOCKS + (j ^ (2 * z)))] * dmid[:, at] - resid[:, at] * back
        ).astype(BF16)


def attend_back_kernel(n, place, *rest):
    pieces, (w_ref, prob_ref, q_ref, k_ref, v_ref, raw_ref, gains_ref, cos_ref, sin_ref,
             dqkv_ref, dgq_ref, dgk_ref, dbr_ref) = rest[:n], rest[n:]
    z = place[0]
    size = pieces[0].shape[0]
    for k in range(n):
        frm = z ^ k
        for j in range(BLOCKS):
            b = place[1 + j]
            dbr_ref[rows_of(frm, size), j * LANE:(j + 1) * LANE] = pieces[k][:, lanes(b ^ (2 * frm))]
    here = dqkv_ref.shape[1]
    dctx = mm(dbr_ref[...], w_ref[:, here:]).astype(BF16)
    qw, kw = q_ref.shape[1], k_ref.shape[1]
    heads, groups = qw // HD, kw // HD
    length = dbr_ref.shape[0]
    cosine, sine = cos_ref[...], sin_ref[...]

    def back(grad, h, gain):
        grad = grad * cosine - pltpu.roll(grad, HD // 2, 1) * sine
        value = raw_ref[:, h * HD:(h + 1) * HD]
        factor = lax.rsqrt(jnp.mean(value * value, axis=-1, keepdims=True) + EPSILON)
        inner = jnp.sum(grad * gain * value, axis=-1, keepdims=True)
        out = factor * gain * grad - value * (factor * factor * factor) * inner / HD
        return out.astype(BF16), jnp.sum(grad * value * factor, axis=0, keepdims=True)

    dgq = dgk = None
    for g in range(groups):
        dk = dv = None
        keys = k_ref[:, g * HD:(g + 1) * HD]
        vals = v_ref[:, g * HD:(g + 1) * HD]
        for h in range(g * heads // groups, (g + 1) * heads // groups):
            hs = slice(h * HD, (h + 1) * HD)
            p = prob_ref[h * length:(h + 1) * length, :]
            dp = mm_nt(dctx[:, hs], vals)
            delta = jnp.sum(p * dp, axis=-1, keepdims=True)
            ds = (p * (dp - delta)).astype(BF16)
            dq, gain_part = back(mm(ds, keys) * HD ** (-0.5), h, gain_of(gains_ref, 0))
            dqkv_ref[:, hs] = dq
            dgq = gain_part if dgq is None else dgq + gain_part
            dk_h = mm_tn(ds, q_ref[:, hs])
            dv_h = mm_tn(p.astype(BF16), dctx[:, hs])
            dk = dk_h if dk is None else dk + dk_h
            dv = dv_h if dv is None else dv + dv_h
        dk, gain_part = back(dk * HD ** (-0.5), heads + g, gain_of(gains_ref, 1))
        dgk = gain_part if dgk is None else dgk + gain_part
        dqkv_ref[:, qw + g * HD:qw + (g + 1) * HD] = dk
        dqkv_ref[:, qw + kw + g * HD:qw + kw + (g + 1) * HD] = dv.astype(BF16)
    dgq_ref[...] = dgq
    dgk_ref[...] = dgk


def weight_grad_kernel(norm_ref, dqkv_ref, dbr_ref, ctx_ref, gz_ref, *outs):
    half = D // 2
    here = dqkv_ref.shape[1]
    step = half // len(outs)
    for left, right, cols in ((norm_ref, dqkv_ref, slice(0, here)), (dbr_ref, ctx_ref, slice(here, None))):
        other = mm_tn(left[:, half:], right[...]).astype(BF16)
        for i, out in enumerate(outs):
            out[0, :, cols] = other[i * step:(i + 1) * step, :]
        gz_ref[0, :, cols] = mm_tn(left[:, :half], right[...])


def input_grad_kernel(n, count, place, dqkv_ref, w_ref, x_ref, gains_ref, *rest):
    units, rest = rest[:count], rest[count:]
    (dg2_ref, dgq_ref, dgk_ref), outs, (gain_ref, dn_ref, term_ref) = rest[:3], rest[3:n + 3], rest[n + 3:]
    z = place[0]
    dn_ref[...] = mm_nt(dqkv_ref[...], w_ref[:, :dqkv_ref.shape[1]])
    x = x_ref[...].astype(F32)
    r1 = lax.rsqrt(jnp.mean(x * x, axis=-1, keepdims=True) + EPSILON)
    inner = None
    for j in range(BLOCKS):
        b = place[1 + j]
        dn = dn_ref[:, j * LANE:(j + 1) * LANE]
        xb = x_ref[:, lanes(b ^ (2 * z))].astype(F32)
        part = dn * gains_ref[:, lanes(b)] * xb
        inner = part if inner is None else inner + part
        gain_ref[:, lanes(b)] = jnp.sum(dn * xb * r1, axis=0, keepdims=True)
    inner = jnp.sum(inner, axis=-1, keepdims=True)
    back = r1 * r1 * r1 * inner / D
    for j in range(BLOCKS):
        b = place[1 + j]
        at = lanes(b ^ (2 * z))
        xb = x_ref[:, at].astype(F32)
        term_ref[:, at] = r1 * gains_ref[:, lanes(b)] * dn_ref[:, j * LANE:(j + 1) * LANE] - xb * back
    width = outs[0].shape[1]
    length = x.shape[0]
    gain_ref[:, D:2 * D] = dg2_ref[...]
    gain_ref[:, 2 * D:2 * D + HD] = dgq_ref[...]
    gain_ref[:, 2 * D + HD:2 * D + 2 * HD] = dgk_ref[...]
    gain_ref[:, 2 * D + 2 * HD:] = jnp.zeros((1, GAIN_ROWS * width - 2 * D - 2 * HD), F32)
    gain_rows = jnp.concatenate([gain_ref[:, i * width:(i + 1) * width] for i in range(GAIN_ROWS)], axis=0)
    for k, out in enumerate(outs):
        out[length:length + GAIN_ROWS, :] = gain_rows.astype(out.dtype)
        out[:length, :] = term_ref[:, k * width:(k + 1) * width].astype(out.dtype)
    if count:
        base, size = length + GAIN_ROWS, units[0].shape[1]
        for i in range(3):
            total = plane_total(units, i)
            for k, out in enumerate(outs):
                out[base + i * size:base + (i + 1) * size, :] = total[:, k * width:(k + 1) * width].astype(out.dtype)


def gain_kernel(base, *rest):
    terms, out_ref = rest[:-1], rest[-1]
    total = terms[0][base:base + GAIN_ROWS, :].astype(F32)
    for term in terms[1:]:
        total = total + term[base:base + GAIN_ROWS, :].astype(F32)
    out_ref[...] = total


def act_kernel(n, place, *rest):
    pieces, terms, downs, (out_ref, grad_ref) = rest[:n], rest[n:2 * n], rest[2 * n:3 * n], rest[3 * n:]
    z = place[0]
    length, width = out_ref.shape
    size = pieces[0].shape[0]
    total = downs[0][...].astype(F32)
    for term in downs[1:]:
        total = total + term[...].astype(F32)
    out_ref[...] = total.astype(BF16)
    for k in range(n):
        at = rows_of(z ^ k, size)
        total = terms[0][at, :].astype(F32)
        for term in terms[1:]:
            total = total + term[at, :].astype(F32)
        grad_ref[at, :] = pieces[k][:, k * width:(k + 1) * width].astype(F32) + total


def body(sizes, act_in, act_cot, segments, positions, gains, gains_first, gains_second,
         query_weight, query_first, query_second, key_weight, key_first, key_second,
         value_weight, value_first, value_second, output_weight, output_first, output_second,
         gate_weight, gate_first, gate_second, up_weight, up_first, up_second,
         down_weight, down_first, down_second):
    n_dp, n_row, n_col = sizes
    n_plane = n_dp * n_col
    paired = n_dp == 2 and n_col == 4
    z = lax.axis_index("row").astype(jnp.int32)
    p = lax.axis_index(PLANE).astype(jnp.int32)

    def over_row(value, k):
        return lax.ppermute(value, "row", [(i, i ^ k) for i in range(n_row)])

    def over_plane(value, k):
        return lax.ppermute(value, PLANE, [(i, i ^ k) for i in range(n_plane)])

    def gather_row(value):
        return [value] + [over_row(value, k) for k in range(1, n_row)]

    def scatter_row(values):
        return [values[0]] + [over_row(values[k], k) for k in range(1, n_row)]

    def near_plane(value, axis=0):
        if not paired:
            return lax.all_gather(value, PLANE, axis=axis, tiled=True)
        return jnp.concatenate([value] + [over_plane(value, k) for k in (2, 4, 6)], axis=axis)

    def far_plane(same, axis=0):
        if not paired:
            return tuple(jnp.split(same, 2, axis=axis))
        return same, over_plane(same, 1)

    def gather_plane(value, axis=0):
        return far_plane(near_plane(value, axis), axis)

    def scatter_plane(same, others):
        if not paired:
            whole = jnp.concatenate([part.astype(F32) for part in (same, *others)], axis=1)
            return [lax.psum_scatter(whole, PLANE, scatter_dimension=1, tiled=True)], (), ()
        lead, size, cols = same.shape
        size, half = size // 4, cols // 2
        keep, keep_x, keep_y, send_x, send_y = call(
            pair_sum_kernel,
            [shape((lead, size, cols), F32)] + [shape((lead, size, half), F32)] * 2
            + [shape((2 * lead, size, half), BF16)] * 2,
            same, *[over_plane(part, 1) for part in others])
        got_x, got_y = over_plane(send_x, 2), over_plane(send_y, 4)
        last_x, last_y = call(relay_sum_kernel, [shape((lead, size, half), BF16)] * 2, keep_x, keep_y, got_x, got_y)
        return [keep, got_x, got_y, over_plane(last_x, 2), over_plane(last_y, 4)], (send_x, send_y), (last_x, last_y)

    def sum_plane(value, first):
        if not paired:
            return lax.psum(value, PLANE)
        value = after(value + over_plane(value, 1), first)
        return value + over_plane(value, 2) + over_plane(value, 4) + over_plane(value, 6)

    order = jnp.array([0, 2, 4, 6, 1, 3, 5, 7], jnp.int32) ^ p if paired else jnp.arange(BLOCKS, dtype=jnp.int32)
    place = jnp.concatenate([z[None], order])

    length, width = act_in.shape
    size = length // n_row
    qw, kw = query_weight.shape[1], key_weight.shape[1]
    rows = query_weight.shape[0]
    units = gate_weight.shape[1]
    gain = gains[None, :]
    cols = 2 * qw + 2 * kw
    share = units // n_row
    small = share % 16 != 0
    if small:
        w_here = jnp.concatenate([query_weight, key_weight, value_weight, output_weight], axis=1).astype(BF16)[None]
        joined = jnp.stack([gate_weight, up_weight, down_weight]).astype(BF16).transpose(0, 2, 1)
        parts = [lax.dynamic_slice_in_dim(joined, (z ^ k) * share, share, 1) for k in range(n_row)]
        units_mine = jnp.concatenate(scatter_row(parts), axis=2)
        xs = gather_row(jnp.concatenate([act_in, act_cot], axis=0))
    else:
        w_here, *xs = call(
            functools.partial(pack_kernel, n_row),
            [shape((1, rows, cols), BF16)] + [shape((2 * length + 3 * share, width), BF16)] * n_row,
            query_weight, key_weight, value_weight, output_weight, act_in, act_cot,
            gate_weight, up_weight, down_weight, hbm=9, limit=59,
            scratch=[pltpu.VMEM((rows, w), F32) for w in (qw, kw, kw, qw)] + [pltpu.VMEM((length, width), BF16)] * 2
            + [pltpu.VMEM((width, units), F32)] * 3 + [pltpu.VMEM((units, width), BF16), pltpu.SemaphoreType.DMA((9,))])
        xs = scatter_row(xs)
    if paired:
        near = [w_here] + [over_plane(w_here, k) for k in (2, 4, 6)]
    else:
        near = list(jnp.split(lax.all_gather(w_here, PLANE, axis=1, tiled=True), 2, axis=1))
    cosine, sine, mask = call(
        tables_kernel, [shape((length, HD), F32)] * 2 + [shape((length, length), F32)],
        positions[None, :], segments[None, :])
    near[-1] = after(near[-1], mask)
    w_parts = near + [over_plane(part, 1) for part in near] if paired else near

    heads = qw // HD
    context, probs, queries, keys, values, raw, normed, x_row, cot_row, w_proj = call(
        functools.partial(attend_kernel, n_row),
        [shape((length, qw), BF16), shape((heads * length, length), F32), shape((length, qw), BF16),
         shape((length, kw), BF16), shape((length, kw), BF16), shape((length, qw + kw), F32),
         shape((length, D), BF16), shape((length, D), BF16), shape((length, D), BF16),
         shape((D, 2 * qw + 2 * kw), BF16)],
        place, *xs, *w_parts, gain, cosine, sine, mask, scalars=1, limit=ATTEND_LIMIT)
    if not small:
        (units_mine,) = call(functools.partial(join_kernel, n_row), [shape((3, share, D), BF16)],
                             *xs)
    units_near = near_plane(units_mine, axis=1)
    terms = call(
        branch_kernel,
        [shape((size, D), F32)] + [shape((size, D), BF16)] * (n_row - 1),
        place, context, w_proj,
        scalars=1, scratch=[pltpu.VMEM((length, D), F32)])
    terms = scatter_row(terms)
    resid, mid = call(
        functools.partial(mid_kernel, n_row),
        [shape((size, D), F32), shape((size, D), BF16)],
        place, x_row, gain, *terms, scalars=1)

    mids = gather_row(mid)
    units_z, units_o = far_plane(after(units_near, mid), axis=1)
    here = 2 * units_z.shape[1]
    *dmid_terms, mid_all, hidden, d_units = call(
        functools.partial(units_kernel, n_row),
        [shape((size, D), F32 if k == 0 else BF16) for k in range(n_row)]
        + [shape((length, D), BF16), shape((length, here), BF16), shape((2, length, here), BF16)],
        place, cot_row, units_z, units_o, *mids,
        scalars=1, scratch=[pltpu.VMEM((length, D), F32)])
    dmid_terms = scatter_row(dmid_terms)
    unit_grad_z, unit_grad_o = call(
        units_grad_kernel, [shape(units_z.shape, BF16)] * 2,
        cot_row, mid_all, hidden, d_units)
    if paired:
        unit_pair = call(
            block_sum_kernel, [shape((3, share, D), F32 if i == 0 else BF16) for i in range(4)],
            unit_grad_z, over_plane(unit_grad_o, 1))
        resid = after(resid, unit_pair[1])
    else:
        unit_pair = scatter_plane(unit_grad_z, [unit_grad_o])[0]
    branch_grad, mid_gain_grad = call(
        functools.partial(mid_back_kernel, n_row),
        [shape((size, D), BF16), shape((1, D), F32)],
        place, resid, cot_row, gain, *dmid_terms,
        scalars=1, scratch=[pltpu.VMEM((size, D), F32)])

    unit_terms = unit_pair[:1]
    if paired:
        unit_terms = [unit_pair[0]] + [over_plane(after(unit_pair[i], branch_grad), k) for i, k in ((1, 2), (2, 4))]
    pieces = gather_row(branch_grad)
    if paired:
        unit_terms.append(over_plane(after(unit_pair[3], *pieces), 6))
    down_terms = call(
        functools.partial(down_kernel, n_row),
        [shape((length, width), F32 if k == 0 else BF16) for k in range(n_row)],
        place, hidden, units_z, units_o, resid,
        scalars=1, scratch=[pltpu.VMEM((length, D), F32)])
    down_terms = scatter_row([after(term, *pieces) for term in down_terms])
    dqkv, query_gain_grad, key_gain_grad, dbranch = call(
        functools.partial(attend_back_kernel, n_row),
        [shape((length, qw + 2 * kw), BF16), shape((1, HD), F32), shape((1, HD), F32), shape((length, D), BF16)],
        place, *pieces, w_proj, probs, queries, keys, values, raw, gain, cosine, sine, scalars=1)
    proj_grad, *proj_others = call(
        weight_grad_kernel, [shape((1, D // 2, cols), F32)] + [shape((1, D // 8, cols), BF16)] * 4,
        normed, after(dqkv, *down_terms, *unit_terms[1:]), dbranch, context)
    proj_terms, _, sent = scatter_plane(proj_grad, proj_others)
    merged = [] if small else unit_terms
    *in_terms, _ = call(
        functools.partial(input_grad_kernel, n_row, len(merged)),
        [shape((length + GAIN_ROWS + 3 * share * bool(merged), width), F32 if k == 0 else BF16)
         for k in range(n_row)]
        + [shape((1, GAIN_ROWS * width), F32)],
        place, dqkv, w_proj, x_row, gain, *merged, mid_gain_grad, query_gain_grad, key_gain_grad,
        scalars=1, scratch=[pltpu.VMEM((length, D), F32)] * 2)
    in_terms = scatter_row(in_terms)
    def update(terms, *states):
        return call(functools.partial(update_kernel, len(terms), len(states) // 3),
                    [shape(state.shape, F32) for state in states], *terms, *states, limit=UPDATE_LIMIT)

    new_proj = update(proj_terms, query_weight, query_first, query_second, key_weight, key_first, key_second,
                      value_weight, value_first, value_second, output_weight, output_first, output_second)

    (gains_grad,) = call(functools.partial(gain_kernel, length), [shape((GAIN_ROWS, width), F32)],
                        after(in_terms[0], new_proj[0]), *in_terms[1:])
    act_out, act_grad = call(
        functools.partial(act_kernel, n_row), [shape((length, width), BF16), shape((length, width), F32)],
        place, *pieces, *in_terms, *down_terms, scalars=1)
    gains_grad = sum_plane(gains_grad, act_out).reshape(-1)[:2 * D + 2 * HD]
    states = (gate_weight, gate_first, gate_second, up_weight, up_first, up_second,
              down_weight, down_first, down_second)
    if small:
        unit_parts = scatter_row(jnp.split(unit_terms[0].astype(BF16), n_row, axis=2))
        whole = jnp.zeros((3, units, width), F32)
        for k, part in enumerate(unit_parts):
            whole = lax.dynamic_update_slice_in_dim(whole, part.astype(F32), (z ^ k) * share, 1)
        new_units = []
        for i in range(3):
            new_units += adamw(*states[3 * i:3 * i + 3], whole[i].T, MATRIX_RATE, MATRIX_DECAY)
    else:
        new_units = call(functools.partial(units_update_kernel, n_row), [shape((width, units), F32)] * 9,
                         place, *in_terms, *states, limit=UPDATE_LIMIT,
                         scalars=1, scratch=[pltpu.VMEM((units, width), F32)])

    return (
        act_out,
        act_grad,
        *adamw(gains, gains_first, gains_second, gains_grad, GAIN_RATE, 0.0),
        *new_proj,
        *new_units,
    )


def solution(mesh):
    token, proj, unit = P(PLANE, "row"), P(PLANE, "row"), P("row", PLANE)
    sizes = (mesh.shape["dp"], mesh.shape["row"], mesh.shape["col"])
    return jax.shard_map(
        functools.partial(body, sizes),
        mesh=mesh,
        in_specs=(token, token, P(PLANE), P(PLANE)) + (P(),) * 3 + (proj,) * 12 + (unit,) * 9,
        out_specs=(token, token) + (P(),) * 3 + (proj,) * 12 + (unit,) * 9,
        check_vma=False,
    )
```

```python
import functools
import math

import jax
import jax.numpy as jnp
from jax import lax
from jax.experimental import pallas as pl
from jax.experimental.pallas import tpu as pltpu
from jax.sharding import PartitionSpec as P

D = 1024
HD = 128
STEP = 10

EPSILON = 1e-06
THETA_BASE = 1000000.0
BETA_FIRST = 0.9
BETA_SECOND = 0.95
ADAM_EPSILON = 1e-08
MATRIX_RATE = 0.04
MATRIX_DECAY = 0.1
GAIN_RATE = 0.5
MASK_VALUE = -1e30
LANE = 128
BLOCKS = D // LANE
ATTEND_LIMIT = 28
UPDATE_LIMIT = 16
GAIN_ROWS = 16
PLANE = ("dp", "col")
F32 = jnp.float32
BF16 = jnp.bfloat16


def mm(left, right):
    return jnp.dot(left, right, preferred_element_type=F32)


def mm_nt(left, right):
    return lax.dot_general(left, right, (((1,), (1,)), ((), ())), preferred_element_type=F32)


def mm_tn(left, right):
    return lax.dot_general(left, right, (((0,), (0,)), ((), ())), preferred_element_type=F32)


def lanes(block):
    return pl.ds(pl.multiple_of(block * LANE, LANE), LANE)


def rows_of(block, size):
    return pl.ds(pl.multiple_of(block * size, size), size)


def call(kernel, outs, *args, scalars=0, scratch=(), hbm=0, ties=0, limit=16):
    vmem = pl.BlockSpec(memory_space=pltpu.VMEM)
    smem = pl.BlockSpec(memory_space=pltpu.SMEM)
    return pl.pallas_call(
        kernel,
        out_shape=list(outs),
        in_specs=[smem] * scalars + [pl.BlockSpec(memory_space=pltpu.HBM)] * hbm
        + [vmem] * (len(args) - scalars - hbm - ties) + [pl.BlockSpec(memory_space=pl.ANY)] * ties,
        out_specs=[vmem] * len(outs),
        scratch_shapes=list(scratch),
        name=(kernel.func if hasattr(kernel, "func") else kernel).__name__,
        compiler_params=pltpu.CompilerParams(vmem_limit_bytes=limit << 20),
        cost_estimate=pl.CostEstimate(flops=1, bytes_accessed=1, transcendentals=0),
    )(*args)


def after(value, *others):
    return lax.optimization_barrier((value, *others))[0]


def shape(dims, dtype):
    return jax.ShapeDtypeStruct(tuple(dims), dtype)


def adamw(weight, first, second, grad, rate, decay):
    first_new = BETA_FIRST * first + (1.0 - BETA_FIRST) * grad
    second_new = BETA_SECOND * second + (1.0 - BETA_SECOND) * grad * grad
    first_hat = first_new * (1.0 / (1.0 - BETA_FIRST**STEP))
    second_hat = second_new * (1.0 / (1.0 - BETA_SECOND**STEP))
    weight_new = weight - rate * (
        first_hat / (jnp.sqrt(second_hat) + ADAM_EPSILON) + decay * weight
    )
    return (weight_new, first_new, second_new)


def gain_of(gains_ref, which):
    at = 2 * D + which * HD
    return gains_ref[:, at:at + HD]


def tables_kernel(pos_ref, seg_ref, cos_ref, sin_ref, mask_ref):
    length, half = pos_ref.shape[1], HD // 2
    column = jnp.broadcast_to(pos_ref[...].astype(F32), (HD, length)).T
    lane = lax.broadcasted_iota(jnp.int32, (1, HD), 1)
    step = (lane & (half - 1)).astype(F32) * (2.0 / HD)
    angle = column * jnp.exp(step * -math.log(THETA_BASE))
    cos_ref[...] = jnp.cos(angle)
    sine = jnp.sin(angle)
    sin_ref[...] = jnp.where(lane < half, -sine, sine)
    seg = jnp.broadcast_to(seg_ref[...].astype(F32), (length, length))
    i = lax.broadcasted_iota(jnp.int32, (length, length), 0)
    j = lax.broadcasted_iota(jnp.int32, (length, length), 1)
    mask_ref[...] = jnp.where((seg == seg.T) & (j <= i), 1.0, 0.0)


def attend_kernel(n, place, *rest):
    blocks = len(rest) - n - 13
    xs, ws, (gains_ref, cos_ref, sin_ref, mask_ref, ctx_ref, prob_ref, q_ref, k_ref, v_ref, raw_ref, norm_ref, x_ref,
             w_ref) = rest[:n], rest[n:n + blocks], rest[n + blocks:]
    height = D // blocks
    for i, w in enumerate(ws):
        w_ref[i * height:(i + 1) * height, :] = w[0]
    z = place[0]
    part = D // n
    for k in range(n):
        x_ref[:, k * part:(k + 1) * part] = xs[k][:x_ref.shape[0], :]
    x = x_ref[...].astype(F32)
    r1 = lax.rsqrt(jnp.mean(x * x, axis=-1, keepdims=True) + EPSILON)
    for j in range(BLOCKS):
        b = place[1 + j]
        block = x_ref[:, lanes(b ^ (2 * z))].astype(F32)
        norm_ref[:, j * LANE:(j + 1) * LANE] = (block * r1 * gains_ref[:, lanes(b)]).astype(BF16)
    qw, kw = q_ref.shape[1], k_ref.shape[1]
    qkv = mm(norm_ref[...], w_ref[:, :qw + 2 * kw])
    raw_ref[...] = qkv[:, :qw + kw]
    v_ref[...] = qkv[:, qw + kw:].astype(BF16)
    cosine, sine = cos_ref[...], sin_ref[...]
    for h in range((qw + kw) // HD):
        part = qkv[:, h * HD:(h + 1) * HD]
        is_q = h * HD < qw
        gain = gain_of(gains_ref, 0 if is_q else 1)
        part = part * lax.rsqrt(jnp.mean(part * part, axis=-1, keepdims=True) + EPSILON) * gain
        part = (part * cosine + pltpu.roll(part, HD // 2, 1) * sine).astype(BF16)
        if is_q:
            q_ref[:, h * HD:(h + 1) * HD] = part
        else:
            at = h * HD - qw
            k_ref[:, at:at + HD] = part
    length = x.shape[0]
    allowed = mask_ref[...] > 0.5
    heads, groups = qw // HD, kw // HD
    for h in range(heads):
        g = h * groups // heads
        s = mm_nt(q_ref[:, h * HD:(h + 1) * HD], k_ref[:, g * HD:(g + 1) * HD]) * HD ** (-0.5)
        s = jnp.where(allowed, s, MASK_VALUE)
        peak = jnp.max(s, axis=-1, keepdims=True)
        total = peak + jnp.log(jnp.sum(jnp.exp(s - peak), axis=-1, keepdims=True))
        p = jnp.exp(s - total)
        prob_ref[h * length:(h + 1) * length, :] = p
        ctx_ref[:, h * HD:(h + 1) * HD] = mm(p.astype(BF16), v_ref[:, g * HD:(g + 1) * HD]).astype(BF16)


def branch_kernel(place, ctx_ref, w_ref, own_ref, *rest):
    sends, scratch = rest[:-1], rest[-1]
    z = place[0]
    here = w_ref.shape[1] - ctx_ref.shape[1]
    scratch[...] = mm_nt(ctx_ref[...], w_ref[:, here:])
    size = own_ref.shape[0]
    for k, out in enumerate((own_ref,) + sends):
        to = z ^ k
        for j in range(BLOCKS):
            b = place[1 + j]
            out[:, lanes(b ^ (2 * to))] = scratch[rows_of(to, size), j * LANE:(j + 1) * LANE].astype(out.dtype)


def mid_kernel(n, place, x_ref, gains_ref, *rest):
    terms, (resid_ref, mid_ref) = rest[:n], rest[n:]
    z = place[0]
    size = resid_ref.shape[0]
    resid = x_ref[rows_of(z, size), :].astype(F32)
    total = terms[0][...].astype(F32)
    for term in terms[1:]:
        total = total + term[...].astype(F32)
    resid = resid + total
    resid_ref[...] = resid
    scale = lax.rsqrt(jnp.mean(resid * resid, axis=-1, keepdims=True) + EPSILON)
    for j in range(BLOCKS):
        at = slice(j * LANE, (j + 1) * LANE)
        mid_ref[:, at] = (resid[:, at] * scale * gains_ref[:, lanes(BLOCKS + (j ^ (2 * z)))]).astype(BF16)


def units_math(gate, up, dhidden):
    sigmoid = jax.nn.sigmoid(gate)
    hidden = (gate * sigmoid * up).astype(BF16)
    dgate = (dhidden * up * sigmoid * (1.0 + gate * (1.0 - sigmoid))).astype(BF16)
    dup = (dhidden * gate * sigmoid).astype(BF16)
    return hidden, dgate, dup


def units_kernel(n, place, wz_ref, wo_ref, *rest):
    cots, pieces, outs = rest[:n], rest[n:2 * n], rest[2 * n:3 * n]
    mid_ref, hid_ref, dgu_ref, cot_ref, dmid_ref = rest[3 * n:]
    z = place[0]
    size = pieces[0].shape[0]
    part = D // n
    for k in range(n):
        for q in range(n):
            mid_ref[rows_of(z ^ k, size), q * part:(q + 1) * part] = (
                pieces[k][:, (q ^ k) * part:((q ^ k) + 1) * part])
        cot_ref[:, k * part:(k + 1) * part] = cots[k][...]
    mid = mid_ref[...]
    cot = cot_ref[...]
    units = wz_ref.shape[1]
    for i, w in enumerate((wz_ref, wo_ref)):
        hidden, dgate, dup = units_math(mm_nt(mid, w[0]), mm_nt(mid, w[1]), mm_nt(cot, w[2]))
        at = slice(i * units, (i + 1) * units)
        hid_ref[:, at] = hidden
        dgu_ref[0, :, at] = dgate
        dgu_ref[1, :, at] = dup
        term = mm(dgate, w[0]) + mm(dup, w[1])
        dmid_ref[...] = term if i == 0 else dmid_ref[...] + term
    for k, out in enumerate(outs):
        out[...] = dmid_ref[rows_of(z ^ k, size), :].astype(out.dtype)


def units_grad_kernel(cot_ref, mid_ref, hid_ref, dgu_ref, gz_ref, go_ref):
    units = gz_ref.shape[1]
    for i, g in ((1, go_ref), (0, gz_ref)):
        at = slice(i * units, (i + 1) * units)
        g[0] = mm_tn(dgu_ref[0, :, at], mid_ref[...]).astype(g.dtype)
        g[1] = mm_tn(dgu_ref[1, :, at], mid_ref[...]).astype(g.dtype)
        g[2] = mm_tn(hid_ref[:, at], cot_ref[...]).astype(g.dtype)


def down_kernel(n, place, hid_ref, wz_ref, wo_ref, resid_ref, *rest):
    outs, total_ref = rest[:n], rest[n]
    units = wz_ref.shape[1]
    size = resid_ref.shape[0]
    total_ref[...] = mm(hid_ref[:, :units], wz_ref[2]) + mm(hid_ref[:, units:], wo_ref[2])
    own = rows_of(place[0], size)
    total_ref[own, :] = total_ref[own, :] + resid_ref[...]
    width = outs[0].shape[1]
    for k, out in enumerate(outs):
        out[...] = total_ref[:, k * width:(k + 1) * width].astype(out.dtype)


def pack_kernel(n, *rest):
    z = lax.axis_index("row")
    sources, out_ref, outs, buffers = rest[:8], rest[8], rest[9:9 + n], rest[9 + n:]
    (*held, scratch, sems) = buffers
    copies = [pltpu.make_async_copy(src, dst, sems.at[i]) for i, (src, dst) in enumerate(zip(sources, held))]
    for copy in copies:
        copy.start()
    at = 0
    for copy, ref in zip(copies[:4], held[:4]):
        copy.wait()
        out_ref[0, :, at:at + ref.shape[1]] = ref[...].astype(BF16)
        at += ref.shape[1]
    x = held[4]
    length = x.shape[0]
    size = (outs[0].shape[0] - length) // 3
    copies[4].wait()
    for out in outs:
        out[:length, :] = x[...]
    for i, (copy, ref) in enumerate(zip(copies[5:], held[5:])):
        copy.wait()
        scratch[...] = ref[...].T.astype(BF16)
        for k, out in enumerate(outs):
            out[length + i * size:length + (i + 1) * size, :] = scratch[rows_of(z ^ k, size), :]


def join_kernel(n, *rest):
    pieces, out_ref = rest[:n], rest[-1]
    size, width = out_ref.shape[1], pieces[0].shape[1]
    length = pieces[0].shape[0] - 3 * size
    for k, piece in enumerate(pieces):
        for i in range(3):
            out_ref[i, :, k * width:(k + 1) * width] = piece[length + i * size:length + (i + 1) * size, :]


def pair_sum_kernel(own_ref, *rest):
    others, (keep_ref, keep_x, keep_y, send_x, send_y) = rest[:-5], rest[-5:]
    lead, size, cols = keep_ref.shape
    half = cols // 2

    def block(i, at):
        rows = slice(i * size, (i + 1) * size)
        other = others[0][:, rows, at] if len(others) == 1 else others[i][:, :, at]
        return own_ref[:, rows, at].astype(F32) + other.astype(F32)

    first, second = slice(0, half), slice(half, cols)
    send_x[:lead] = block(1, first).astype(BF16)
    send_x[lead:] = block(3, first).astype(BF16)
    send_y[:lead] = block(2, second).astype(BF16)
    send_y[lead:] = block(3, second).astype(BF16)
    keep_ref[...] = block(0, slice(0, cols))
    keep_x[...] = block(1, second)
    keep_y[...] = block(2, first)


def block_sum_kernel(own_ref, other_ref, *outs):
    size = outs[0].shape[1]
    for i, out in enumerate(outs):
        rows = slice(i * size, (i + 1) * size)
        out[...] = (own_ref[:, rows, :].astype(F32) + other_ref[:, rows, :].astype(F32)).astype(out.dtype)


def relay_sum_kernel(keep_x, keep_y, got_x, got_y, send_x, send_y):
    lead = keep_x.shape[0]
    send_y[...] = (keep_y[...] + got_x[lead:].astype(F32)).astype(BF16)
    send_x[...] = (keep_x[...] + got_y[lead:].astype(F32)).astype(BF16)


def plane_total(terms, i):
    if len(terms) != 5:
        total = terms[0][i].astype(F32)
        for term in terms[1:]:
            total = total + term[i].astype(F32)
        return total
    keep, got_x, got_y, last_x, last_y = terms
    half = keep.shape[2] // 2
    first = keep[i, :, :half] + (got_x[i].astype(F32) + last_y[i].astype(F32))
    second = keep[i, :, half:] + (got_y[i].astype(F32) + last_x[i].astype(F32))
    return jnp.concatenate([first, second], axis=1)


def units_update_kernel(n, place, *rest):
    pieces, states, outs, scratch = rest[:n], rest[n:n + 9], rest[n + 9:n + 18], rest[n + 18]
    size = scratch.shape[0] // n
    base = pieces[0].shape[0] - 3 * size
    for i in range(3):
        for k in range(n):
            scratch[rows_of(place[0] ^ k, size), :] = pieces[k][base + i * size:base + (i + 1) * size, :].astype(F32)
        w, m, v = (ref[...] for ref in states[3 * i:3 * i + 3])
        for ref, value in zip(outs[3 * i:3 * i + 3], adamw(w, m, v, scratch[...].T, MATRIX_RATE, MATRIX_DECAY)):
            ref[...] = value


def update_kernel(n, count, *rest):
    terms, states, outs = rest[:n], rest[n:n + 3 * count], rest[n + 3 * count:]
    total = plane_total(terms, 0)
    at = 0
    for i in range(count):
        w, m, v = (ref[...] for ref in states[3 * i:3 * i + 3])
        grad = total[:, at:at + w.shape[1]]
        at += w.shape[1]
        for ref, value in zip(outs[3 * i:3 * i + 3], adamw(w, m, v, grad, MATRIX_RATE, MATRIX_DECAY)):
            ref[...] = value


def mid_back_kernel(n, place, resid_ref, cot_ref, gains_ref, *rest):
    terms, (grad_ref, gain_ref, dmid_ref) = rest[:n], rest[n:]
    z = place[0]
    part = D // n
    for k, term in enumerate(terms):
        for q in range(n):
            at = slice(q * part, (q + 1) * part)
            value = term[:, (q ^ k) * part:((q ^ k) + 1) * part].astype(F32)
            dmid_ref[:, at] = value if k == 0 else dmid_ref[:, at] + value
    dmid = dmid_ref[...]
    resid = resid_ref[...]
    cot = cot_ref[rows_of(z, resid.shape[0]), :].astype(F32)
    r2 = lax.rsqrt(jnp.mean(resid * resid, axis=-1, keepdims=True) + EPSILON)
    inner = None
    for j in range(BLOCKS):
        at = slice(j * LANE, (j + 1) * LANE)
        b = j ^ (2 * z)
        part = dmid[:, at] * gains_ref[:, lanes(BLOCKS + b)] * resid[:, at]
        inner = part if inner is None else inner + part
        gain_ref[:, lanes(b)] = jnp.sum(dmid[:, at] * resid[:, at] * r2, axis=0, keepdims=True)
    inner = jnp.sum(inner, axis=-1, keepdims=True)
    back = r2 * r2 * r2 * inner / D
    for j in range(BLOCKS):
        at = slice(j * LANE, (j + 1) * LANE)
        grad_ref[:, at] = (
            cot[:, at] + r2 * gains_ref[:, lanes(BLOCKS + (j ^ (2 * z)))] * dmid[:, at] - resid[:, at] * back
        ).astype(BF16)


def attend_back_kernel(n, place, *rest):
    pieces, (w_ref, prob_ref, q_ref, k_ref, v_ref, raw_ref, gains_ref, cos_ref, sin_ref,
             dqkv_ref, dgq_ref, dgk_ref, dbr_ref) = rest[:n], rest[n:]
    z = place[0]
    size = pieces[0].shape[0]
    for k in range(n):
        frm = z ^ k
        for j in range(BLOCKS):
            b = place[1 + j]
            dbr_ref[rows_of(frm, size), j * LANE:(j + 1) * LANE] = pieces[k][:, lanes(b ^ (2 * frm))]
    here = dqkv_ref.shape[1]
    dctx = mm(dbr_ref[...], w_ref[:, here:]).astype(BF16)
    qw, kw = q_ref.shape[1], k_ref.shape[1]
    heads, groups = qw // HD, kw // HD
    length = dbr_ref.shape[0]
    cosine, sine = cos_ref[...], sin_ref[...]

    def back(grad, h, gain):
        grad = grad * cosine - pltpu.roll(grad, HD // 2, 1) * sine
        value = raw_ref[:, h * HD:(h + 1) * HD]
        factor = lax.rsqrt(jnp.mean(value * value, axis=-1, keepdims=True) + EPSILON)
        inner = jnp.sum(grad * gain * value, axis=-1, keepdims=True)
        out = factor * gain * grad - value * (factor * factor * factor) * inner / HD
        return out.astype(BF16), jnp.sum(grad * value * factor, axis=0, keepdims=True)

    dgq = dgk = None
    for g in range(groups):
        dk = dv = None
        keys = k_ref[:, g * HD:(g + 1) * HD]
        vals = v_ref[:, g * HD:(g + 1) * HD]
        for h in range(g * heads // groups, (g + 1) * heads // groups):
            hs = slice(h * HD, (h + 1) * HD)
            p = prob_ref[h * length:(h + 1) * length, :]
            dp = mm_nt(dctx[:, hs], vals)
            delta = jnp.sum(p * dp, axis=-1, keepdims=True)
            ds = (p * (dp - delta)).astype(BF16)
            dq, gain_part = back(mm(ds, keys) * HD ** (-0.5), h, gain_of(gains_ref, 0))
            dqkv_ref[:, hs] = dq
            dgq = gain_part if dgq is None else dgq + gain_part
            dk_h = mm_tn(ds, q_ref[:, hs])
            dv_h = mm_tn(p.astype(BF16), dctx[:, hs])
            dk = dk_h if dk is None else dk + dk_h
            dv = dv_h if dv is None else dv + dv_h
        dk, gain_part = back(dk * HD ** (-0.5), heads + g, gain_of(gains_ref, 1))
        dgk = gain_part if dgk is None else dgk + gain_part
        dqkv_ref[:, qw + g * HD:qw + (g + 1) * HD] = dk
        dqkv_ref[:, qw + kw + g * HD:qw + kw + (g + 1) * HD] = dv.astype(BF16)
    dgq_ref[...] = dgq
    dgk_ref[...] = dgk


def weight_grad_kernel(norm_ref, dqkv_ref, dbr_ref, ctx_ref, gz_ref, *outs):
    half = D // 2
    here = dqkv_ref.shape[1]
    step = half // len(outs)
    for left, right, cols in ((norm_ref, dqkv_ref, slice(0, here)), (dbr_ref, ctx_ref, slice(here, None))):
        other = mm_tn(left[:, half:], right[...]).astype(BF16)
        for i, out in enumerate(outs):
            out[0, :, cols] = other[i * step:(i + 1) * step, :]
        gz_ref[0, :, cols] = mm_tn(left[:, :half], right[...])


def input_grad_kernel(n, count, place, dqkv_ref, w_ref, x_ref, gains_ref, *rest):
    units, rest = rest[:count], rest[count:]
    (dg2_ref, dgq_ref, dgk_ref), outs, (gain_ref, dn_ref, term_ref) = rest[:3], rest[3:n + 3], rest[n + 3:]
    z = place[0]
    dn_ref[...] = mm_nt(dqkv_ref[...], w_ref[:, :dqkv_ref.shape[1]])
    x = x_ref[...].astype(F32)
    r1 = lax.rsqrt(jnp.mean(x * x, axis=-1, keepdims=True) + EPSILON)
    inner = None
    for j in range(BLOCKS):
        b = place[1 + j]
        dn = dn_ref[:, j * LANE:(j + 1) * LANE]
        xb = x_ref[:, lanes(b ^ (2 * z))].astype(F32)
        part = dn * gains_ref[:, lanes(b)] * xb
        inner = part if inner is None else inner + part
        gain_ref[:, lanes(b)] = jnp.sum(dn * xb * r1, axis=0, keepdims=True)
    inner = jnp.sum(inner, axis=-1, keepdims=True)
    back = r1 * r1 * r1 * inner / D
    for j in range(BLOCKS):
        b = place[1 + j]
        at = lanes(b ^ (2 * z))
        xb = x_ref[:, at].astype(F32)
        term_ref[:, at] = r1 * gains_ref[:, lanes(b)] * dn_ref[:, j * LANE:(j + 1) * LANE] - xb * back
    width = outs[0].shape[1]
    length = x.shape[0]
    gain_ref[:, D:2 * D] = dg2_ref[...]
    gain_ref[:, 2 * D:2 * D + HD] = dgq_ref[...]
    gain_ref[:, 2 * D + HD:2 * D + 2 * HD] = dgk_ref[...]
    gain_ref[:, 2 * D + 2 * HD:] = jnp.zeros((1, GAIN_ROWS * width - 2 * D - 2 * HD), F32)
    gain_rows = jnp.concatenate([gain_ref[:, i * width:(i + 1) * width] for i in range(GAIN_ROWS)], axis=0)
    for k, out in enumerate(outs):
        out[length:length + GAIN_ROWS, :] = gain_rows.astype(out.dtype)
        out[:length, :] = term_ref[:, k * width:(k + 1) * width].astype(out.dtype)
    if count:
        base, size = length + GAIN_ROWS, units[0].shape[1]
        for i in range(3):
            total = plane_total(units, i)
            for k, out in enumerate(outs):
                out[base + i * size:base + (i + 1) * size, :] = total[:, k * width:(k + 1) * width].astype(out.dtype)


def gain_kernel(base, *rest):
    terms, out_ref = rest[:-1], rest[-1]
    total = terms[0][base:base + GAIN_ROWS, :].astype(F32)
    for term in terms[1:]:
        total = total + term[base:base + GAIN_ROWS, :].astype(F32)
    out_ref[...] = total


def act_kernel(n, place, *rest):
    pieces, terms, downs, (out_ref, grad_ref) = rest[:n], rest[n:2 * n], rest[2 * n:3 * n], rest[3 * n:]
    z = place[0]
    length, width = out_ref.shape
    size = pieces[0].shape[0]
    total = downs[0][...].astype(F32)
    for term in downs[1:]:
        total = total + term[...].astype(F32)
    out_ref[...] = total.astype(BF16)
    for k in range(n):
        at = rows_of(z ^ k, size)
        total = terms[0][at, :].astype(F32)
        for term in terms[1:]:
            total = total + term[at, :].astype(F32)
        grad_ref[at, :] = pieces[k][:, k * width:(k + 1) * width].astype(F32) + total


def body(sizes, act_in, act_cot, segments, positions, gains, gains_first, gains_second,
         query_weight, query_first, query_second, key_weight, key_first, key_second,
         value_weight, value_first, value_second, output_weight, output_first, output_second,
         gate_weight, gate_first, gate_second, up_weight, up_first, up_second,
         down_weight, down_first, down_second):
    n_dp, n_row, n_col = sizes
    n_plane = n_dp * n_col
    paired = n_dp == 2 and n_col == 4
    z = lax.axis_index("row").astype(jnp.int32)
    p = lax.axis_index(PLANE).astype(jnp.int32)

    def over_row(value, k):
        return lax.ppermute(value, "row", [(i, i ^ k) for i in range(n_row)])

    def over_plane(value, k):
        return lax.ppermute(value, PLANE, [(i, i ^ k) for i in range(n_plane)])

    def gather_row(value):
        return [value] + [over_row(value, k) for k in range(1, n_row)]

    def scatter_row(values):
        return [values[0]] + [over_row(values[k], k) for k in range(1, n_row)]

    def near_plane(value, axis=0):
        if not paired:
            return lax.all_gather(value, PLANE, axis=axis, tiled=True)
        return jnp.concatenate([value] + [over_plane(value, k) for k in (2, 4, 6)], axis=axis)

    def far_plane(same, axis=0):
        if not paired:
            return tuple(jnp.split(same, 2, axis=axis))
        return same, over_plane(same, 1)

    def gather_plane(value, axis=0):
        return far_plane(near_plane(value, axis), axis)

    def scatter_plane(same, others):
        if not paired:
            whole = jnp.concatenate([part.astype(F32) for part in (same, *others)], axis=1)
            return [lax.psum_scatter(whole, PLANE, scatter_dimension=1, tiled=True)], (), ()
        lead, size, cols = same.shape
        size, half = size // 4, cols // 2
        keep, keep_x, keep_y, send_x, send_y = call(
            pair_sum_kernel,
            [shape((lead, size, cols), F32)] + [shape((lead, size, half), F32)] * 2
            + [shape((2 * lead, size, half), BF16)] * 2,
            same, *[over_plane(part, 1) for part in others])
        got_x, got_y = over_plane(send_x, 2), over_plane(send_y, 4)
        last_x, last_y = call(relay_sum_kernel, [shape((lead, size, half), BF16)] * 2, keep_x, keep_y, got_x, got_y)
        return [keep, got_x, got_y, over_plane(last_x, 2), over_plane(last_y, 4)], (send_x, send_y), (last_x, last_y)

    def sum_plane(value, first):
        if not paired:
            return lax.psum(value, PLANE)
        value = after(value + over_plane(value, 1), first)
        return value + over_plane(value, 2) + over_plane(value, 4) + over_plane(value, 6)

    order = jnp.array([0, 2, 4, 6, 1, 3, 5, 7], jnp.int32) ^ p if paired else jnp.arange(BLOCKS, dtype=jnp.int32)
    place = jnp.concatenate([z[None], order])

    length, width = act_in.shape
    size = length // n_row
    qw, kw = query_weight.shape[1], key_weight.shape[1]
    rows = query_weight.shape[0]
    units = gate_weight.shape[1]
    gain = gains[None, :]
    cols = 2 * qw + 2 * kw
    share = units // n_row
    small = share % 16 != 0
    if small:
        w_here = jnp.concatenate([query_weight, key_weight, value_weight, output_weight], axis=1).astype(BF16)[None]
        joined = jnp.stack([gate_weight, up_weight, down_weight]).astype(BF16).transpose(0, 2, 1)
        parts = [lax.dynamic_slice_in_dim(joined, (z ^ k) * share, share, 1) for k in range(n_row)]
        units_mine = jnp.concatenate(scatter_row(parts), axis=2)
        xs = gather_row(act_in)
    else:
        w_here, *xs = call(
            functools.partial(pack_kernel, n_row),
            [shape((1, rows, cols), BF16)] + [shape((length + 3 * share, width), BF16)] * n_row,
            query_weight, key_weight, value_weight, output_weight, act_in,
            gate_weight, up_weight, down_weight, hbm=8, limit=59,
            scratch=[pltpu.VMEM((rows, w), F32) for w in (qw, kw, kw, qw)] + [pltpu.VMEM((length, width), BF16)]
            + [pltpu.VMEM((width, units), F32)] * 3 + [pltpu.VMEM((units, width), BF16), pltpu.SemaphoreType.DMA((8,))])
        xs = scatter_row(xs)
    if paired:
        near = [w_here] + [over_plane(w_here, k) for k in (2, 4, 6)]
    else:
        near = list(jnp.split(lax.all_gather(w_here, PLANE, axis=1, tiled=True), 2, axis=1))
    cosine, sine, mask = call(
        tables_kernel, [shape((length, HD), F32)] * 2 + [shape((length, length), F32)],
        positions[None, :], segments[None, :])
    near[-1] = after(near[-1], mask)
    w_parts = near + [over_plane(part, 1) for part in near] if paired else near

    heads = qw // HD
    context, probs, queries, keys, values, raw, normed, x_row, w_proj = call(
        functools.partial(attend_kernel, n_row),
        [shape((length, qw), BF16), shape((heads * length, length), F32), shape((length, qw), BF16),
         shape((length, kw), BF16), shape((length, kw), BF16), shape((length, qw + kw), F32),
         shape((length, D), BF16), shape((length, D), BF16),
         shape((D, 2 * qw + 2 * kw), BF16)],
        place, *xs, *w_parts, gain, cosine, sine, mask, scalars=1, limit=ATTEND_LIMIT)
    if not small:
        (units_mine,) = call(functools.partial(join_kernel, n_row), [shape((3, share, D), BF16)],
                             *xs)
    units_near = near_plane(units_mine, axis=1)
    terms = call(
        branch_kernel,
        [shape((size, D), F32)] + [shape((size, D), BF16)] * (n_row - 1),
        place, context, w_proj,
        scalars=1, scratch=[pltpu.VMEM((length, D), F32)])
    terms = scatter_row(terms)
    resid, mid = call(
        functools.partial(mid_kernel, n_row),
        [shape((size, D), F32), shape((size, D), BF16)],
        place, x_row, gain, *terms, scalars=1)

    mids = gather_row(mid)
    units_z, units_o = far_plane(after(units_near, *mids), axis=1)
    cots = gather_row(after(act_cot, mid))
    here = 2 * units_z.shape[1]
    *dmid_terms, mid_all, hidden, d_units, cot_row = call(
        functools.partial(units_kernel, n_row),
        [shape((size, D), F32 if k == 0 else BF16) for k in range(n_row)]
        + [shape((length, D), BF16), shape((length, here), BF16), shape((2, length, here), BF16),
           shape((length, D), BF16)],
        place, units_z, units_o, *cots, *mids,
        scalars=1, scratch=[pltpu.VMEM((length, D), F32)])
    dmid_terms = scatter_row(dmid_terms)
    unit_grad_z, unit_grad_o = call(
        units_grad_kernel, [shape(units_z.shape, BF16)] * 2,
        cot_row, mid_all, hidden, d_units)
    if paired:
        unit_pair = call(
            block_sum_kernel, [shape((3, share, D), F32 if i == 0 else BF16) for i in range(4)],
            unit_grad_z, over_plane(unit_grad_o, 1))
        resid = after(resid, unit_pair[1])
    else:
        unit_pair = scatter_plane(unit_grad_z, [unit_grad_o])[0]
    branch_grad, mid_gain_grad = call(
        functools.partial(mid_back_kernel, n_row),
        [shape((size, D), BF16), shape((1, D), F32)],
        place, resid, cot_row, gain, *dmid_terms,
        scalars=1, scratch=[pltpu.VMEM((size, D), F32)])

    unit_terms = unit_pair[:1]
    if paired:
        unit_terms = [unit_pair[0]] + [over_plane(after(unit_pair[i], branch_grad), k) for i, k in ((1, 2), (2, 4))]
    pieces = gather_row(branch_grad)
    if paired:
        unit_terms.append(over_plane(after(unit_pair[3], *pieces), 6))
    down_terms = call(
        functools.partial(down_kernel, n_row),
        [shape((length, width), F32 if k == 0 else BF16) for k in range(n_row)],
        place, hidden, units_z, units_o, resid,
        scalars=1, scratch=[pltpu.VMEM((length, D), F32)])
    down_terms = scatter_row([after(term, *pieces) for term in down_terms])
    dqkv, query_gain_grad, key_gain_grad, dbranch = call(
        functools.partial(attend_back_kernel, n_row),
        [shape((length, qw + 2 * kw), BF16), shape((1, HD), F32), shape((1, HD), F32), shape((length, D), BF16)],
        place, *pieces, w_proj, probs, queries, keys, values, raw, gain, cosine, sine, scalars=1)
    proj_grad, *proj_others = call(
        weight_grad_kernel, [shape((1, D // 2, cols), F32)] + [shape((1, D // 8, cols), BF16)] * 4,
        normed, after(dqkv, *down_terms, *unit_terms[1:]), dbranch, context)
    proj_terms, _, sent = scatter_plane(proj_grad, proj_others)
    merged = [] if small else unit_terms
    *in_terms, _ = call(
        functools.partial(input_grad_kernel, n_row, len(merged)),
        [shape((length + GAIN_ROWS + 3 * share * bool(merged), width), F32 if k == 0 else BF16)
         for k in range(n_row)]
        + [shape((1, GAIN_ROWS * width), F32)],
        place, dqkv, w_proj, x_row, gain, *merged, mid_gain_grad, query_gain_grad, key_gain_grad,
        scalars=1, scratch=[pltpu.VMEM((length, D), F32)] * 2)
    in_terms = scatter_row(in_terms)
    def update(terms, *states):
        return call(functools.partial(update_kernel, len(terms), len(states) // 3),
                    [shape(state.shape, F32) for state in states], *terms, *states, limit=UPDATE_LIMIT)

    new_proj = update(proj_terms, query_weight, query_first, query_second, key_weight, key_first, key_second,
                      value_weight, value_first, value_second, output_weight, output_first, output_second)

    (gains_grad,) = call(functools.partial(gain_kernel, length), [shape((GAIN_ROWS, width), F32)],
                        after(in_terms[0], new_proj[0]), *in_terms[1:])
    act_out, act_grad = call(
        functools.partial(act_kernel, n_row), [shape((length, width), BF16), shape((length, width), F32)],
        place, *pieces, *in_terms, *down_terms, scalars=1)
    gains_grad = sum_plane(gains_grad, act_out).reshape(-1)[:2 * D + 2 * HD]
    states = (gate_weight, gate_first, gate_second, up_weight, up_first, up_second,
              down_weight, down_first, down_second)
    if small:
        unit_parts = scatter_row(jnp.split(unit_terms[0].astype(BF16), n_row, axis=2))
        whole = jnp.zeros((3, units, width), F32)
        for k, part in enumerate(unit_parts):
            whole = lax.dynamic_update_slice_in_dim(whole, part.astype(F32), (z ^ k) * share, 1)
        new_units = []
        for i in range(3):
            new_units += adamw(*states[3 * i:3 * i + 3], whole[i].T, MATRIX_RATE, MATRIX_DECAY)
    else:
        new_units = call(functools.partial(units_update_kernel, n_row), [shape((width, units), F32)] * 9,
                         place, *in_terms, *states, limit=UPDATE_LIMIT,
                         scalars=1, scratch=[pltpu.VMEM((units, width), F32)])

    return (
        act_out,
        act_grad,
        *adamw(gains, gains_first, gains_second, gains_grad, GAIN_RATE, 0.0),
        *new_proj,
        *new_units,
    )


def solution(mesh):
    token, proj, unit = P(PLANE, "row"), P(PLANE, "row"), P("row", PLANE)
    sizes = (mesh.shape["dp"], mesh.shape["row"], mesh.shape["col"])
    return jax.shard_map(
        functools.partial(body, sizes),
        mesh=mesh,
        in_specs=(token, token, P(PLANE), P(PLANE)) + (P(),) * 3 + (proj,) * 12 + (unit,) * 9,
        out_specs=(token, token) + (P(),) * 3 + (proj,) * 12 + (unit,) * 9,
        check_vma=False,
    )
```

```python
import functools
import math

import jax
import jax.numpy as jnp
from jax import lax
from jax.experimental import pallas as pl
from jax.experimental.pallas import tpu as pltpu
from jax.sharding import PartitionSpec as P

D = 1024
HD = 128
STEP = 10

EPSILON = 1e-06
THETA_BASE = 1000000.0
BETA_FIRST = 0.9
BETA_SECOND = 0.95
ADAM_EPSILON = 1e-08
MATRIX_RATE = 0.04
MATRIX_DECAY = 0.1
GAIN_RATE = 0.5
MASK_VALUE = -1e30
LANE = 128
BLOCKS = D // LANE
ATTEND_LIMIT = 28
UPDATE_LIMIT = 16
GAIN_ROWS = 16
PLANE = ("dp", "col")
F32 = jnp.float32
BF16 = jnp.bfloat16


def mm(left, right):
    return jnp.dot(left, right, preferred_element_type=F32)


def mm_nt(left, right):
    return lax.dot_general(left, right, (((1,), (1,)), ((), ())), preferred_element_type=F32)


def mm_tn(left, right):
    return lax.dot_general(left, right, (((0,), (0,)), ((), ())), preferred_element_type=F32)


def lanes(block):
    return pl.ds(pl.multiple_of(block * LANE, LANE), LANE)


def rows_of(block, size):
    return pl.ds(pl.multiple_of(block * size, size), size)


def call(kernel, outs, *args, scalars=0, scratch=(), hbm=0, ties=0, limit=16):
    vmem = pl.BlockSpec(memory_space=pltpu.VMEM)
    smem = pl.BlockSpec(memory_space=pltpu.SMEM)
    return pl.pallas_call(
        kernel,
        out_shape=list(outs),
        in_specs=[smem] * scalars + [pl.BlockSpec(memory_space=pltpu.HBM)] * hbm
        + [vmem] * (len(args) - scalars - hbm - ties) + [pl.BlockSpec(memory_space=pl.ANY)] * ties,
        out_specs=[vmem] * len(outs),
        scratch_shapes=list(scratch),
        name=(kernel.func if hasattr(kernel, "func") else kernel).__name__,
        compiler_params=pltpu.CompilerParams(vmem_limit_bytes=limit << 20),
        cost_estimate=pl.CostEstimate(flops=1, bytes_accessed=1, transcendentals=0),
    )(*args)


def after(value, *others):
    return lax.optimization_barrier((value, *others))[0]


def shape(dims, dtype):
    return jax.ShapeDtypeStruct(tuple(dims), dtype)


def adamw(weight, first, second, grad, rate, decay):
    first_new = BETA_FIRST * first + (1.0 - BETA_FIRST) * grad
    second_new = BETA_SECOND * second + (1.0 - BETA_SECOND) * grad * grad
    step = first_new * (rate / (1.0 - BETA_FIRST**STEP))
    scale = jnp.sqrt(second_new * (1.0 / (1.0 - BETA_SECOND**STEP))) + ADAM_EPSILON
    weight_new = weight * (1.0 - rate * decay) - step / scale
    return (weight_new, first_new, second_new)


def gain_of(gains_ref, which):
    at = 2 * D + which * HD
    return gains_ref[:, at:at + HD]


def tables_kernel(pos_ref, seg_ref, cos_ref, sin_ref, mask_ref):
    length, half = pos_ref.shape[1], HD // 2
    column = jnp.broadcast_to(pos_ref[...].astype(F32), (HD, length)).T
    lane = lax.broadcasted_iota(jnp.int32, (1, HD), 1)
    step = (lane & (half - 1)).astype(F32) * (2.0 / HD)
    angle = column * jnp.exp(step * -math.log(THETA_BASE))
    cos_ref[...] = jnp.cos(angle)
    sine = jnp.sin(angle)
    sin_ref[...] = jnp.where(lane < half, -sine, sine)
    seg = jnp.broadcast_to(seg_ref[...].astype(F32), (length, length))
    i = lax.broadcasted_iota(jnp.int32, (length, length), 0)
    j = lax.broadcasted_iota(jnp.int32, (length, length), 1)
    mask_ref[...] = jnp.where((seg == seg.T) & (j <= i), 1.0, 0.0)


def attend_kernel(n, place, *rest):
    blocks = len(rest) - n - 13
    xs, ws, (gains_ref, cos_ref, sin_ref, mask_ref, ctx_ref, prob_ref, q_ref, k_ref, v_ref, raw_ref, norm_ref, x_ref,
             w_ref) = rest[:n], rest[n:n + blocks], rest[n + blocks:]
    height = D // blocks
    for i, w in enumerate(ws):
        w_ref[i * height:(i + 1) * height, :] = w[0]
    z = place[0]
    part = D // n
    for k in range(n):
        x_ref[:, k * part:(k + 1) * part] = xs[k][:x_ref.shape[0], :]
    x = x_ref[...].astype(F32)
    r1 = lax.rsqrt(jnp.mean(x * x, axis=-1, keepdims=True) + EPSILON)
    for j in range(BLOCKS):
        b = place[1 + j]
        block = x_ref[:, lanes(b ^ (2 * z))].astype(F32)
        norm_ref[:, j * LANE:(j + 1) * LANE] = (block * r1 * gains_ref[:, lanes(b)]).astype(BF16)
    qw, kw = q_ref.shape[1], k_ref.shape[1]
    qkv = mm(norm_ref[...], w_ref[:, :qw + 2 * kw])
    raw_ref[...] = qkv[:, :qw + kw]
    v_ref[...] = qkv[:, qw + kw:].astype(BF16)
    cosine, sine = cos_ref[...], sin_ref[...]
    for h in range((qw + kw) // HD):
        part = qkv[:, h * HD:(h + 1) * HD]
        is_q = h * HD < qw
        gain = gain_of(gains_ref, 0 if is_q else 1)
        part = part * lax.rsqrt(jnp.mean(part * part, axis=-1, keepdims=True) + EPSILON) * gain
        part = (part * cosine + pltpu.roll(part, HD // 2, 1) * sine).astype(BF16)
        if is_q:
            q_ref[:, h * HD:(h + 1) * HD] = part
        else:
            at = h * HD - qw
            k_ref[:, at:at + HD] = part
    length = x.shape[0]
    allowed = mask_ref[...] > 0.5
    heads, groups = qw // HD, kw // HD
    for h in range(heads):
        g = h * groups // heads
        s = mm_nt(q_ref[:, h * HD:(h + 1) * HD], k_ref[:, g * HD:(g + 1) * HD]) * HD ** (-0.5)
        s = jnp.where(allowed, s, MASK_VALUE)
        peak = jnp.max(s, axis=-1, keepdims=True)
        total = peak + jnp.log(jnp.sum(jnp.exp(s - peak), axis=-1, keepdims=True))
        p = jnp.exp(s - total)
        prob_ref[h * length:(h + 1) * length, :] = p
        ctx_ref[:, h * HD:(h + 1) * HD] = mm(p.astype(BF16), v_ref[:, g * HD:(g + 1) * HD]).astype(BF16)


def branch_kernel(place, ctx_ref, w_ref, own_ref, *rest):
    sends, scratch = rest[:-1], rest[-1]
    z = place[0]
    here = w_ref.shape[1] - ctx_ref.shape[1]
    scratch[...] = mm_nt(ctx_ref[...], w_ref[:, here:])
    size = own_ref.shape[0]
    for k, out in enumerate((own_ref,) + sends):
        to = z ^ k
        for j in range(BLOCKS):
            b = place[1 + j]
            out[:, lanes(b ^ (2 * to))] = scratch[rows_of(to, size), j * LANE:(j + 1) * LANE].astype(out.dtype)


def mid_kernel(n, place, x_ref, gains_ref, *rest):
    terms, (resid_ref, mid_ref) = rest[:n], rest[n:]
    z = place[0]
    size = resid_ref.shape[0]
    resid = x_ref[rows_of(z, size), :].astype(F32)
    total = terms[0][...].astype(F32)
    for term in terms[1:]:
        total = total + term[...].astype(F32)
    resid = resid + total
    resid_ref[...] = resid
    scale = lax.rsqrt(jnp.mean(resid * resid, axis=-1, keepdims=True) + EPSILON)
    for j in range(BLOCKS):
        at = slice(j * LANE, (j + 1) * LANE)
        mid_ref[:, at] = (resid[:, at] * scale * gains_ref[:, lanes(BLOCKS + (j ^ (2 * z)))]).astype(BF16)


def units_math(gate, up, dhidden):
    sigmoid = jax.nn.sigmoid(gate)
    hidden = (gate * sigmoid * up).astype(BF16)
    dgate = (dhidden * up * sigmoid * (1.0 + gate * (1.0 - sigmoid))).astype(BF16)
    dup = (dhidden * gate * sigmoid).astype(BF16)
    return hidden, dgate, dup


def units_kernel(n, place, wz_ref, wo_ref, *rest):
    cots, pieces, outs = rest[:n], rest[n:2 * n], rest[2 * n:3 * n]
    mid_ref, hid_ref, dgu_ref, cot_ref, dmid_ref = rest[3 * n:]
    z = place[0]
    size = pieces[0].shape[0]
    part = D // n
    for k in range(n):
        for q in range(n):
            mid_ref[rows_of(z ^ k, size), q * part:(q + 1) * part] = (
                pieces[k][:, (q ^ k) * part:((q ^ k) + 1) * part])
        cot_ref[:, k * part:(k + 1) * part] = cots[k][...]
    mid = mid_ref[...]
    cot = cot_ref[...]
    units = wz_ref.shape[1]
    for i, w in enumerate((wz_ref, wo_ref)):
        hidden, dgate, dup = units_math(mm_nt(mid, w[0]), mm_nt(mid, w[1]), mm_nt(cot, w[2]))
        at = slice(i * units, (i + 1) * units)
        hid_ref[:, at] = hidden
        dgu_ref[0, :, at] = dgate
        dgu_ref[1, :, at] = dup
        term = mm(dgate, w[0]) + mm(dup, w[1])
        dmid_ref[...] = term if i == 0 else dmid_ref[...] + term
    for k, out in enumerate(outs):
        out[...] = dmid_ref[rows_of(z ^ k, size), :].astype(out.dtype)


def units_grad_kernel(cot_ref, mid_ref, hid_ref, dgu_ref, gz_ref, go_ref):
    units = gz_ref.shape[1]
    for i, g in ((1, go_ref), (0, gz_ref)):
        at = slice(i * units, (i + 1) * units)
        g[0] = mm_tn(dgu_ref[0, :, at], mid_ref[...]).astype(g.dtype)
        g[1] = mm_tn(dgu_ref[1, :, at], mid_ref[...]).astype(g.dtype)
        g[2] = mm_tn(hid_ref[:, at], cot_ref[...]).astype(g.dtype)


def down_kernel(n, place, hid_ref, wz_ref, wo_ref, resid_ref, *rest):
    outs, total_ref = rest[:n], rest[n]
    units = wz_ref.shape[1]
    size = resid_ref.shape[0]
    total_ref[...] = mm(hid_ref[:, :units], wz_ref[2]) + mm(hid_ref[:, units:], wo_ref[2])
    own = rows_of(place[0], size)
    total_ref[own, :] = total_ref[own, :] + resid_ref[...]
    width = outs[0].shape[1]
    for k, out in enumerate(outs):
        out[...] = total_ref[:, k * width:(k + 1) * width].astype(out.dtype)


def pack_kernel(n, *rest):
    z = lax.axis_index("row")
    sources, out_ref, outs, buffers = rest[:8], rest[8], rest[9:9 + n], rest[9 + n:]
    (*held, scratch, sems) = buffers
    copies = [pltpu.make_async_copy(src, dst, sems.at[i]) for i, (src, dst) in enumerate(zip(sources, held))]
    for copy in copies:
        copy.start()
    at = 0
    for copy, ref in zip(copies[:4], held[:4]):
        copy.wait()
        out_ref[0, :, at:at + ref.shape[1]] = ref[...].astype(BF16)
        at += ref.shape[1]
    x = held[4]
    length = x.shape[0]
    size = (outs[0].shape[0] - length) // 3
    copies[4].wait()
    for out in outs:
        out[:length, :] = x[...]
    for i, (copy, ref) in enumerate(zip(copies[5:], held[5:])):
        copy.wait()
        scratch[...] = ref[...].T.astype(BF16)
        for k, out in enumerate(outs):
            out[length + i * size:length + (i + 1) * size, :] = scratch[rows_of(z ^ k, size), :]


def join_kernel(n, *rest):
    pieces, out_ref = rest[:n], rest[-1]
    size, width = out_ref.shape[1], pieces[0].shape[1]
    length = pieces[0].shape[0] - 3 * size
    for k, piece in enumerate(pieces):
        for i in range(3):
            out_ref[i, :, k * width:(k + 1) * width] = piece[length + i * size:length + (i + 1) * size, :]


def pair_sum_kernel(own_ref, *rest):
    others, (keep_ref, keep_x, keep_y, send_x, send_y) = rest[:-5], rest[-5:]
    lead, size, cols = keep_ref.shape
    half = cols // 2

    def block(i, at):
        rows = slice(i * size, (i + 1) * size)
        other = others[0][:, rows, at] if len(others) == 1 else others[i][:, :, at]
        return own_ref[:, rows, at].astype(F32) + other.astype(F32)

    first, second = slice(0, half), slice(half, cols)
    send_x[:lead] = block(1, first).astype(BF16)
    send_x[lead:] = block(3, first).astype(BF16)
    send_y[:lead] = block(2, second).astype(BF16)
    send_y[lead:] = block(3, second).astype(BF16)
    keep_ref[...] = block(0, slice(0, cols))
    keep_x[...] = block(1, second)
    keep_y[...] = block(2, first)


def block_sum_kernel(own_ref, other_ref, *outs):
    size = outs[0].shape[1]
    for i, out in enumerate(outs):
        rows = slice(i * size, (i + 1) * size)
        out[...] = (own_ref[:, rows, :].astype(F32) + other_ref[:, rows, :].astype(F32)).astype(out.dtype)


def relay_sum_kernel(keep_x, keep_y, got_x, got_y, send_x, send_y):
    lead = keep_x.shape[0]
    send_y[...] = (keep_y[...] + got_x[lead:].astype(F32)).astype(BF16)
    send_x[...] = (keep_x[...] + got_y[lead:].astype(F32)).astype(BF16)


def plane_total(terms, i):
    if len(terms) != 5:
        total = terms[0][i].astype(F32)
        for term in terms[1:]:
            total = total + term[i].astype(F32)
        return total
    keep, got_x, got_y, last_x, last_y = terms
    half = keep.shape[2] // 2
    first = keep[i, :, :half] + (got_x[i].astype(F32) + last_y[i].astype(F32))
    second = keep[i, :, half:] + (got_y[i].astype(F32) + last_x[i].astype(F32))
    return jnp.concatenate([first, second], axis=1)


def units_update_kernel(n, place, *rest):
    pieces, states, outs, scratch = rest[:n], rest[n:n + 9], rest[n + 9:n + 18], rest[n + 18]
    size = scratch.shape[0] // n
    base = pieces[0].shape[0] - 3 * size
    for i in range(3):
        for k in range(n):
            scratch[rows_of(place[0] ^ k, size), :] = pieces[k][base + i * size:base + (i + 1) * size, :].astype(F32)
        w, m, v = (ref[...] for ref in states[3 * i:3 * i + 3])
        for ref, value in zip(outs[3 * i:3 * i + 3], adamw(w, m, v, scratch[...].T, MATRIX_RATE, MATRIX_DECAY)):
            ref[...] = value


def update_kernel(n, count, *rest):
    terms, states, outs = rest[:n], rest[n:n + 3 * count], rest[n + 3 * count:]
    total = plane_total(terms, 0)
    at = 0
    for i in range(count):
        w, m, v = (ref[...] for ref in states[3 * i:3 * i + 3])
        grad = total[:, at:at + w.shape[1]]
        at += w.shape[1]
        for ref, value in zip(outs[3 * i:3 * i + 3], adamw(w, m, v, grad, MATRIX_RATE, MATRIX_DECAY)):
            ref[...] = value


def mid_back_kernel(n, place, resid_ref, cot_ref, gains_ref, *rest):
    terms, (grad_ref, gain_ref, dmid_ref) = rest[:n], rest[n:]
    z = place[0]
    part = D // n
    for k, term in enumerate(terms):
        for q in range(n):
            at = slice(q * part, (q + 1) * part)
            value = term[:, (q ^ k) * part:((q ^ k) + 1) * part].astype(F32)
            dmid_ref[:, at] = value if k == 0 else dmid_ref[:, at] + value
    dmid = dmid_ref[...]
    resid = resid_ref[...]
    cot = cot_ref[rows_of(z, resid.shape[0]), :].astype(F32)
    r2 = lax.rsqrt(jnp.mean(resid * resid, axis=-1, keepdims=True) + EPSILON)
    inner = None
    for j in range(BLOCKS):
        at = slice(j * LANE, (j + 1) * LANE)
        b = j ^ (2 * z)
        part = dmid[:, at] * gains_ref[:, lanes(BLOCKS + b)] * resid[:, at]
        inner = part if inner is None else inner + part
        gain_ref[:, lanes(b)] = jnp.sum(dmid[:, at] * resid[:, at] * r2, axis=0, keepdims=True)
    inner = jnp.sum(inner, axis=-1, keepdims=True)
    back = r2 * r2 * r2 * inner / D
    for j in range(BLOCKS):
        at = slice(j * LANE, (j + 1) * LANE)
        grad_ref[:, at] = (
            cot[:, at] + r2 * gains_ref[:, lanes(BLOCKS + (j ^ (2 * z)))] * dmid[:, at] - resid[:, at] * back
        ).astype(BF16)


def attend_back_kernel(n, place, *rest):
    pieces, (w_ref, prob_ref, q_ref, k_ref, v_ref, raw_ref, gains_ref, cos_ref, sin_ref,
             dqkv_ref, dgq_ref, dgk_ref, dbr_ref) = rest[:n], rest[n:]
    z = place[0]
    size = pieces[0].shape[0]
    for k in range(n):
        frm = z ^ k
        for j in range(BLOCKS):
            b = place[1 + j]
            dbr_ref[rows_of(frm, size), j * LANE:(j + 1) * LANE] = pieces[k][:, lanes(b ^ (2 * frm))]
    here = dqkv_ref.shape[1]
    dctx = mm(dbr_ref[...], w_ref[:, here:]).astype(BF16)
    qw, kw = q_ref.shape[1], k_ref.shape[1]
    heads, groups = qw // HD, kw // HD
    length = dbr_ref.shape[0]
    cosine, sine = cos_ref[...], sin_ref[...]

    def back(grad, h, gain):
        grad = grad * cosine - pltpu.roll(grad, HD // 2, 1) * sine
        value = raw_ref[:, h * HD:(h + 1) * HD]
        factor = lax.rsqrt(jnp.mean(value * value, axis=-1, keepdims=True) + EPSILON)
        inner = jnp.sum(grad * gain * value, axis=-1, keepdims=True)
        out = factor * gain * grad - value * (factor * factor * factor) * inner / HD
        return out.astype(BF16), jnp.sum(grad * value * factor, axis=0, keepdims=True)

    dgq = dgk = None
    for g in range(groups):
        dk = dv = None
        keys = k_ref[:, g * HD:(g + 1) * HD]
        vals = v_ref[:, g * HD:(g + 1) * HD]
        for h in range(g * heads // groups, (g + 1) * heads // groups):
            hs = slice(h * HD, (h + 1) * HD)
            p = prob_ref[h * length:(h + 1) * length, :]
            dp = mm_nt(dctx[:, hs], vals)
            delta = jnp.sum(p * dp, axis=-1, keepdims=True)
            ds = (p * (dp - delta)).astype(BF16)
            dq, gain_part = back(mm(ds, keys) * HD ** (-0.5), h, gain_of(gains_ref, 0))
            dqkv_ref[:, hs] = dq
            dgq = gain_part if dgq is None else dgq + gain_part
            dk_h = mm_tn(ds, q_ref[:, hs])
            dv_h = mm_tn(p.astype(BF16), dctx[:, hs])
            dk = dk_h if dk is None else dk + dk_h
            dv = dv_h if dv is None else dv + dv_h
        dk, gain_part = back(dk * HD ** (-0.5), heads + g, gain_of(gains_ref, 1))
        dgk = gain_part if dgk is None else dgk + gain_part
        dqkv_ref[:, qw + g * HD:qw + (g + 1) * HD] = dk
        dqkv_ref[:, qw + kw + g * HD:qw + kw + (g + 1) * HD] = dv.astype(BF16)
    dgq_ref[...] = dgq
    dgk_ref[...] = dgk


def weight_grad_kernel(norm_ref, dqkv_ref, dbr_ref, ctx_ref, gz_ref, *outs):
    half = D // 2
    here = dqkv_ref.shape[1]
    step = half // len(outs)
    for left, right, cols in ((norm_ref, dqkv_ref, slice(0, here)), (dbr_ref, ctx_ref, slice(here, None))):
        other = mm_tn(left[:, half:], right[...]).astype(BF16)
        for i, out in enumerate(outs):
            out[0, :, cols] = other[i * step:(i + 1) * step, :]
        gz_ref[0, :, cols] = mm_tn(left[:, :half], right[...])


def input_grad_kernel(n, count, place, dqkv_ref, w_ref, x_ref, gains_ref, *rest):
    units, rest = rest[:count], rest[count:]
    (dg2_ref, dgq_ref, dgk_ref), outs, (gain_ref, dn_ref, term_ref) = rest[:3], rest[3:n + 3], rest[n + 3:]
    z = place[0]
    dn_ref[...] = mm_nt(dqkv_ref[...], w_ref[:, :dqkv_ref.shape[1]])
    x = x_ref[...].astype(F32)
    r1 = lax.rsqrt(jnp.mean(x * x, axis=-1, keepdims=True) + EPSILON)
    inner = None
    for j in range(BLOCKS):
        b = place[1 + j]
        dn = dn_ref[:, j * LANE:(j + 1) * LANE]
        xb = x_ref[:, lanes(b ^ (2 * z))].astype(F32)
        part = dn * gains_ref[:, lanes(b)] * xb
        inner = part if inner is None else inner + part
        gain_ref[:, lanes(b)] = jnp.sum(dn * xb * r1, axis=0, keepdims=True)
    inner = jnp.sum(inner, axis=-1, keepdims=True)
    back = r1 * r1 * r1 * inner / D
    for j in range(BLOCKS):
        b = place[1 + j]
        at = lanes(b ^ (2 * z))
        xb = x_ref[:, at].astype(F32)
        term_ref[:, at] = r1 * gains_ref[:, lanes(b)] * dn_ref[:, j * LANE:(j + 1) * LANE] - xb * back
    width = outs[0].shape[1]
    length = x.shape[0]
    gain_ref[:, D:2 * D] = dg2_ref[...]
    gain_ref[:, 2 * D:2 * D + HD] = dgq_ref[...]
    gain_ref[:, 2 * D + HD:2 * D + 2 * HD] = dgk_ref[...]
    gain_ref[:, 2 * D + 2 * HD:] = jnp.zeros((1, GAIN_ROWS * width - 2 * D - 2 * HD), F32)
    gain_rows = jnp.concatenate([gain_ref[:, i * width:(i + 1) * width] for i in range(GAIN_ROWS)], axis=0)
    for k, out in enumerate(outs):
        out[length:length + GAIN_ROWS, :] = gain_rows.astype(out.dtype)
        out[:length, :] = term_ref[:, k * width:(k + 1) * width].astype(out.dtype)
    if count:
        base, size = length + GAIN_ROWS, units[0].shape[1]
        for i in range(3):
            total = plane_total(units, i)
            for k, out in enumerate(outs):
                out[base + i * size:base + (i + 1) * size, :] = total[:, k * width:(k + 1) * width].astype(out.dtype)


def gain_kernel(base, *rest):
    terms, out_ref = rest[:-1], rest[-1]
    total = terms[0][base:base + GAIN_ROWS, :].astype(F32)
    for term in terms[1:]:
        total = total + term[base:base + GAIN_ROWS, :].astype(F32)
    out_ref[...] = total


def act_kernel(n, place, *rest):
    pieces, terms, downs, (out_ref, grad_ref) = rest[:n], rest[n:2 * n], rest[2 * n:3 * n], rest[3 * n:]
    z = place[0]
    length, width = out_ref.shape
    size = pieces[0].shape[0]
    total = downs[0][...].astype(F32)
    for term in downs[1:]:
        total = total + term[...].astype(F32)
    out_ref[...] = total.astype(BF16)
    for k in range(n):
        at = rows_of(z ^ k, size)
        total = terms[0][at, :].astype(F32)
        for term in terms[1:]:
            total = total + term[at, :].astype(F32)
        grad_ref[at, :] = pieces[k][:, k * width:(k + 1) * width].astype(F32) + total


def body(sizes, act_in, act_cot, segments, positions, gains, gains_first, gains_second,
         query_weight, query_first, query_second, key_weight, key_first, key_second,
         value_weight, value_first, value_second, output_weight, output_first, output_second,
         gate_weight, gate_first, gate_second, up_weight, up_first, up_second,
         down_weight, down_first, down_second):
    n_dp, n_row, n_col = sizes
    n_plane = n_dp * n_col
    paired = n_dp == 2 and n_col == 4
    z = lax.axis_index("row").astype(jnp.int32)
    p = lax.axis_index(PLANE).astype(jnp.int32)

    def over_row(value, k):
        return lax.ppermute(value, "row", [(i, i ^ k) for i in range(n_row)])

    def over_plane(value, k):
        return lax.ppermute(value, PLANE, [(i, i ^ k) for i in range(n_plane)])

    def gather_row(value):
        return [value] + [over_row(value, k) for k in range(1, n_row)]

    def scatter_row(values):
        return [values[0]] + [over_row(values[k], k) for k in range(1, n_row)]

    def near_plane(value, axis=0):
        if not paired:
            return lax.all_gather(value, PLANE, axis=axis, tiled=True)
        return jnp.concatenate([value] + [over_plane(value, k) for k in (2, 4, 6)], axis=axis)

    def far_plane(same, axis=0):
        if not paired:
            return tuple(jnp.split(same, 2, axis=axis))
        return same, over_plane(same, 1)

    def gather_plane(value, axis=0):
        return far_plane(near_plane(value, axis), axis)

    def scatter_plane(same, others):
        if not paired:
            whole = jnp.concatenate([part.astype(F32) for part in (same, *others)], axis=1)
            return [lax.psum_scatter(whole, PLANE, scatter_dimension=1, tiled=True)], (), ()
        lead, size, cols = same.shape
        size, half = size // 4, cols // 2
        keep, keep_x, keep_y, send_x, send_y = call(
            pair_sum_kernel,
            [shape((lead, size, cols), F32)] + [shape((lead, size, half), F32)] * 2
            + [shape((2 * lead, size, half), BF16)] * 2,
            same, *[over_plane(part, 1) for part in others])
        got_x, got_y = over_plane(send_x, 2), over_plane(send_y, 4)
        last_x, last_y = call(relay_sum_kernel, [shape((lead, size, half), BF16)] * 2, keep_x, keep_y, got_x, got_y)
        return [keep, got_x, got_y, over_plane(last_x, 2), over_plane(last_y, 4)], (send_x, send_y), (last_x, last_y)

    def sum_plane(value, first):
        if not paired:
            return lax.psum(value, PLANE)
        value = after(value + over_plane(value, 1), first)
        return value + over_plane(value, 2) + over_plane(value, 4) + over_plane(value, 6)

    order = jnp.array([0, 2, 4, 6, 1, 3, 5, 7], jnp.int32) ^ p if paired else jnp.arange(BLOCKS, dtype=jnp.int32)
    place = jnp.concatenate([z[None], order])

    length, width = act_in.shape
    size = length // n_row
    qw, kw = query_weight.shape[1], key_weight.shape[1]
    rows = query_weight.shape[0]
    units = gate_weight.shape[1]
    gain = gains[None, :]
    cols = 2 * qw + 2 * kw
    share = units // n_row
    small = share % 16 != 0
    if small:
        w_here = jnp.concatenate([query_weight, key_weight, value_weight, output_weight], axis=1).astype(BF16)[None]
        joined = jnp.stack([gate_weight, up_weight, down_weight]).astype(BF16).transpose(0, 2, 1)
        parts = [lax.dynamic_slice_in_dim(joined, (z ^ k) * share, share, 1) for k in range(n_row)]
        units_mine = jnp.concatenate(scatter_row(parts), axis=2)
        xs = gather_row(act_in)
    else:
        w_here, *xs = call(
            functools.partial(pack_kernel, n_row),
            [shape((1, rows, cols), BF16)] + [shape((length + 3 * share, width), BF16)] * n_row,
            query_weight, key_weight, value_weight, output_weight, act_in,
            gate_weight, up_weight, down_weight, hbm=8, limit=59,
            scratch=[pltpu.VMEM((rows, w), F32) for w in (qw, kw, kw, qw)] + [pltpu.VMEM((length, width), BF16)]
            + [pltpu.VMEM((width, units), F32)] * 3 + [pltpu.VMEM((units, width), BF16), pltpu.SemaphoreType.DMA((8,))])
        xs = scatter_row(xs)
    if paired:
        near = [w_here] + [over_plane(w_here, k) for k in (2, 4, 6)]
    else:
        near = list(jnp.split(lax.all_gather(w_here, PLANE, axis=1, tiled=True), 2, axis=1))
    cosine, sine, mask = call(
        tables_kernel, [shape((length, HD), F32)] * 2 + [shape((length, length), F32)],
        positions[None, :], segments[None, :])
    near[-1] = after(near[-1], mask)
    w_parts = near + [over_plane(part, 1) for part in near] if paired else near

    heads = qw // HD
    context, probs, queries, keys, values, raw, normed, x_row, w_proj = call(
        functools.partial(attend_kernel, n_row),
        [shape((length, qw), BF16), shape((heads * length, length), F32), shape((length, qw), BF16),
         shape((length, kw), BF16), shape((length, kw), BF16), shape((length, qw + kw), F32),
         shape((length, D), BF16), shape((length, D), BF16),
         shape((D, 2 * qw + 2 * kw), BF16)],
        place, *xs, *w_parts, gain, cosine, sine, mask, scalars=1, limit=ATTEND_LIMIT)
    if not small:
        (units_mine,) = call(functools.partial(join_kernel, n_row), [shape((3, share, D), BF16)],
                             *xs)
    units_near = near_plane(units_mine, axis=1)
    terms = call(
        branch_kernel,
        [shape((size, D), F32)] + [shape((size, D), BF16)] * (n_row - 1),
        place, context, w_proj,
        scalars=1, scratch=[pltpu.VMEM((length, D), F32)])
    terms = scatter_row(terms)
    resid, mid = call(
        functools.partial(mid_kernel, n_row),
        [shape((size, D), F32), shape((size, D), BF16)],
        place, x_row, gain, *terms, scalars=1)

    mids = gather_row(mid)
    units_z, units_o = far_plane(after(units_near, *mids), axis=1)
    cots = gather_row(after(act_cot, mid))
    here = 2 * units_z.shape[1]
    *dmid_terms, mid_all, hidden, d_units, cot_row = call(
        functools.partial(units_kernel, n_row),
        [shape((size, D), F32 if k == 0 else BF16) for k in range(n_row)]
        + [shape((length, D), BF16), shape((length, here), BF16), shape((2, length, here), BF16),
           shape((length, D), BF16)],
        place, units_z, units_o, *cots, *mids,
        scalars=1, scratch=[pltpu.VMEM((length, D), F32)])
    dmid_terms = scatter_row(dmid_terms)
    unit_grad_z, unit_grad_o = call(
        units_grad_kernel, [shape(units_z.shape, BF16)] * 2,
        cot_row, mid_all, hidden, d_units)
    if paired:
        unit_pair = call(
            block_sum_kernel, [shape((3, share, D), F32 if i == 0 else BF16) for i in range(4)],
            unit_grad_z, over_plane(unit_grad_o, 1))
        resid = after(resid, unit_pair[1])
    else:
        unit_pair = scatter_plane(unit_grad_z, [unit_grad_o])[0]
    branch_grad, mid_gain_grad = call(
        functools.partial(mid_back_kernel, n_row),
        [shape((size, D), BF16), shape((1, D), F32)],
        place, resid, cot_row, gain, *dmid_terms,
        scalars=1, scratch=[pltpu.VMEM((size, D), F32)])

    unit_terms = unit_pair[:1]
    if paired:
        unit_terms = [unit_pair[0]] + [over_plane(after(unit_pair[i], branch_grad), k) for i, k in ((1, 2), (2, 4))]
    pieces = gather_row(branch_grad)
    if paired:
        unit_terms.append(over_plane(after(unit_pair[3], *pieces), 6))
    down_terms = call(
        functools.partial(down_kernel, n_row),
        [shape((length, width), F32 if k == 0 else BF16) for k in range(n_row)],
        place, hidden, units_z, units_o, resid,
        scalars=1, scratch=[pltpu.VMEM((length, D), F32)])
    down_terms = scatter_row([after(term, *pieces) for term in down_terms])
    dqkv, query_gain_grad, key_gain_grad, dbranch = call(
        functools.partial(attend_back_kernel, n_row),
        [shape((length, qw + 2 * kw), BF16), shape((1, HD), F32), shape((1, HD), F32), shape((length, D), BF16)],
        place, *pieces, w_proj, probs, queries, keys, values, raw, gain, cosine, sine, scalars=1)
    proj_grad, *proj_others = call(
        weight_grad_kernel, [shape((1, D // 2, cols), F32)] + [shape((1, D // 8, cols), BF16)] * 4,
        normed, after(dqkv, *down_terms, *unit_terms[1:]), dbranch, context)
    proj_terms, _, sent = scatter_plane(proj_grad, proj_others)
    merged = [] if small else unit_terms
    *in_terms, _ = call(
        functools.partial(input_grad_kernel, n_row, len(merged)),
        [shape((length + GAIN_ROWS + 3 * share * bool(merged), width), F32 if k == 0 else BF16)
         for k in range(n_row)]
        + [shape((1, GAIN_ROWS * width), F32)],
        place, dqkv, w_proj, x_row, gain, *merged, mid_gain_grad, query_gain_grad, key_gain_grad,
        scalars=1, scratch=[pltpu.VMEM((length, D), F32)] * 2)
    in_terms = scatter_row(in_terms)
    def update(terms, *states):
        return call(functools.partial(update_kernel, len(terms), len(states) // 3),
                    [shape(state.shape, F32) for state in states], *terms, *states, limit=UPDATE_LIMIT)

    new_proj = update(proj_terms, query_weight, query_first, query_second, key_weight, key_first, key_second,
                      value_weight, value_first, value_second, output_weight, output_first, output_second)

    (gains_grad,) = call(functools.partial(gain_kernel, length), [shape((GAIN_ROWS, width), F32)],
                        after(in_terms[0], new_proj[0]), *in_terms[1:])
    act_out, act_grad = call(
        functools.partial(act_kernel, n_row), [shape((length, width), BF16), shape((length, width), F32)],
        place, *pieces, *in_terms, *down_terms, scalars=1)
    gains_grad = sum_plane(gains_grad, act_out).reshape(-1)[:2 * D + 2 * HD]
    states = (gate_weight, gate_first, gate_second, up_weight, up_first, up_second,
              down_weight, down_first, down_second)
    if small:
        unit_parts = scatter_row(jnp.split(unit_terms[0].astype(BF16), n_row, axis=2))
        whole = jnp.zeros((3, units, width), F32)
        for k, part in enumerate(unit_parts):
            whole = lax.dynamic_update_slice_in_dim(whole, part.astype(F32), (z ^ k) * share, 1)
        new_units = []
        for i in range(3):
            new_units += adamw(*states[3 * i:3 * i + 3], whole[i].T, MATRIX_RATE, MATRIX_DECAY)
    else:
        new_units = call(functools.partial(units_update_kernel, n_row), [shape((width, units), F32)] * 9,
                         place, *in_terms, *states, limit=UPDATE_LIMIT,
                         scalars=1, scratch=[pltpu.VMEM((units, width), F32)])

    return (
        act_out,
        act_grad,
        *adamw(gains, gains_first, gains_second, gains_grad, GAIN_RATE, 0.0),
        *new_proj,
        *new_units,
    )


def solution(mesh):
    token, proj, unit = P(PLANE, "row"), P(PLANE, "row"), P("row", PLANE)
    sizes = (mesh.shape["dp"], mesh.shape["row"], mesh.shape["col"])
    return jax.shard_map(
        functools.partial(body, sizes),
        mesh=mesh,
        in_specs=(token, token, P(PLANE), P(PLANE)) + (P(),) * 3 + (proj,) * 12 + (unit,) * 9,
        out_specs=(token, token) + (P(),) * 3 + (proj,) * 12 + (unit,) * 9,
        check_vma=False,
    )
```
